256 devices in a mesh: seq: 128 (over y, z_hi, x, core), ch: 2 (over z_lo).
Axes of the slice: x: 4, y: 4, z: 8 (z_hi: 4, z_lo: 2; z = z_hi * 2 + z_lo), core: 2. Of those that a mesh axis runs over, the one named last changes fastest.
Arguments:
- query: float32 [8, 1048576], P(None, ('seq', 'ch')), may hold values from -6 to 6
- key: float32 [8, 1048576], P('ch', 'seq'), may hold values from -6 to 6
- value: float32 [8, 1048576], P('ch', 'seq'), may hold values from -6 to 6
- filters: float32 [8, 1048576], P('ch', 'seq'), may hold values from -0.005859375 to 0.005859375
- short_taps: float32 [2, 8, 3], P(None, 'ch'), may hold values from -3.5 to 3.5
- bias: float32 [8], P('ch'), may hold values from -4 to 4
Outputs:
- mixed_out: float32 [8, 1048576], P(None, ('seq', 'ch'))
The draws below stay inside these ranges and needn't reach their ends.
All inputs are finite; a program needn't handle non-finite values.
Results may differ from the reference program's by a relative error of at most 0.00011.
Values sent between devices are 32-bit elements; how exact they have to be, the bound alone decides.
A program may use at most 64 MiB of HBM per device.

```python
import jax
import jax.numpy as jnp
from jax import lax

SHORT = 3
CHANNELS = 8
TOKENS = 1048576


def levels(stream_key, shape, cuts, least, largest):
    loudness = 1.0
    for dim, blocks in cuts:
        draws = jax.random.uniform(jax.random.fold_in(jax.random.fold_in(stream_key, 6), dim), (blocks,), jnp.float32, least / len(cuts), largest / len(cuts))
        loudness = loudness * jnp.repeat(jnp.exp(draws), shape[dim] // blocks).reshape((-1,) + (1,) * (len(shape) - 1 - dim))
    return loudness


def centred(stream_key, shape, width, limit, pieces=(), held_as=jnp.bfloat16):
    entries = jax.random.normal(stream_key, shape, jnp.float32) * width
    if len(pieces) > 0:
        entries = levels(stream_key, shape, pieces, -0.22, 0.18) * entries
    return jnp.clip(entries, min=-limit, max=limit).astype(held_as)


def setup_inputs(seed: int = 0) -> dict:
    seeds = jax.random.split(jax.random.key(seed), 7)
    return {
        "query": centred(seeds[0], (CHANNELS, TOKENS), 1.0, 6.0, ((1, 256),), jnp.float32),
        "key": centred(seeds[1], (CHANNELS, TOKENS), 1.0, 6.0, ((0, 2), (1, 128)), jnp.float32),
        "value": centred(seeds[2], (CHANNELS, TOKENS), 1.0, 6.0, ((0, 2), (1, 128)), jnp.float32),
        "filters": centred(seeds[3], (CHANNELS, TOKENS), TOKENS ** -0.5, 0.005859375, ((0, 2), (1, 128)), jnp.float32),
        "short_taps": centred(seeds[4], (2, CHANNELS, SHORT), SHORT ** -0.5, 3.5, ((1, 2),), jnp.float32),
        "bias": centred(seeds[5], (CHANNELS,), 1.0, 4.0, ((0, 2),), jnp.float32),
    }


def short_conv(signal, taps):
    span_len = signal.shape[1]
    padded = jnp.pad(signal, ((0, 0), (2, 0)))
    return taps[:, 0:1] * padded[:, 2:] + taps[:, 1:2] * padded[:, 1:span_len + 1] + taps[:, 2:3] * padded[:, 0:span_len]


def long_conv(signal, kernel):
    span_len = signal.shape[-1]
    spectrum = jnp.fft.rfft(signal, 2 * span_len) * jnp.fft.rfft(kernel, 2 * span_len)
    return jnp.fft.irfft(spectrum, 2 * span_len)[:span_len]


def reference(query, key, value, filters, short_taps, bias):
    gated = short_conv(key, short_taps[0]) * short_conv(value, short_taps[1])
    convolved = lax.map(lambda members: long_conv(members[0], members[1]), (gated, filters))
    convolved = convolved.astype(gated.dtype)
    return query * (convolved + bias[:, None] * gated)
```

```python
import functools

import jax
import jax.numpy as jnp
import ml_dtypes
import numpy as np
from jax import lax
from jax.experimental import pallas as pl
from jax.experimental.pallas import tpu as pltpu
from jax.sharding import PartitionSpec as P

MESH = pl.DeviceIdType.MESH
F32 = jnp.float32
BF16 = jnp.bfloat16


def two_parts(table):
    high = table.astype(np.float32).astype(ml_dtypes.bfloat16)
    low = (table - high.astype(np.float64)).astype(np.float32).astype(ml_dtypes.bfloat16)
    return high, low


def as_left(table):
    high, low = two_parts(table)
    return np.concatenate([high, high, low], axis=1)


def as_right(table):
    high, low = two_parts(table)
    return np.concatenate([high, high, low], axis=0)


def make_tables():
    j1, k1 = np.arange(32), np.arange(32)
    lanes = np.arange(128)
    head = 2 * np.pi * np.outer(k1 + 0.5, j1) / 64
    same = np.eye(8)
    step = np.stack([np.cos(head), -np.sin(head)])
    head_in = np.einsum("rkj,ab->rkabj", step, same).reshape(512, 256)
    head_out = np.einsum("rkj,ab->bjrka", step, same).reshape(256, 512)
    turn = np.repeat(2 * np.pi * np.outer(k1 + 0.5, lanes) / 8192, 8, axis=0)
    turn = np.concatenate([np.cos(turn), np.sin(turn)], axis=1).astype(np.float32)
    tail = 2 * np.pi * np.outer(lanes, lanes) / 128
    c, s = np.cos(tail), np.sin(tail)
    tail_in = np.block([[c, -s], [s, c]])
    tail_out = np.block([[c, s], [-s, c]])
    place = np.arange(256).reshape(4, 4, 8, 2).transpose(0, 2, 1, 3).reshape(256)
    nu = np.arange(512)
    phase = 2 * np.pi * np.outer(nu, place) / 512
    block_in = np.concatenate([np.cos(phase), np.sin(phase)], axis=0)
    block_out = []
    for sign in (1, -1):
        wave = np.exp(1j * phase.T) * (1 + sign * 1j * np.exp(-2j * np.pi * nu / 512))[None, :]
        wave = wave * 2.0**-21
        block_out.append(as_left(np.concatenate([wave.real, wave.imag], axis=0)))
    return (
        as_left(head_in),
        as_right(tail_in),
        turn,
        as_left(block_in),
        np.stack(block_out),
        as_right(tail_out),
        as_left(head_out),
    )


def put_split(ref, value, axis):
    high = value.astype(BF16)
    low = (value - high.astype(F32)).astype(BF16)
    n = value.shape[axis]
    for place, part in enumerate((high, low, high)):
        if axis == 0:
            ref[place * n : (place + 1) * n, :] = part
        else:
            ref[:, place * n : (place + 1) * n] = part


def mm(a, b):
    return jnp.dot(a, b, preferred_element_type=F32)


def kernel(
    taps, bias, query, key, value, filt,
    head_in_h, tail_in_h, turn_h, block_in_h, block_out_h, tail_out_h, head_out_h,
    out,
    query_v, key_v, value_v, filt_v,
    head_in, tail_in, turn, block_in, block_out, tail_out, head_out,
    halo, rows, zbuf, sbuf, rbuf, spec, wide, back_s, back_r, done_s, done_r,
    right_a, left_b, right_q, right_i, left_o, right_o,
    load_sem, halo_send, halo_recv, z_send, z_recv, xy_send, xy_recv,
    back_send, back_recv, done_send, done_recv,
):
    seq = lax.axis_index("seq")
    ch = lax.axis_index("ch")
    y = seq // 32
    zh = (seq // 8) % 4
    s = seq % 8
    me = y * 8 + s
    z = zh * 2 + ch

    def xy_device(d):
        return {"seq": (d // 8) * 32 + zh * 8 + d % 8, "ch": ch}

    def z_device(to):
        return {"seq": y * 32 + (to // 2) * 8 + s, "ch": to % 2}

    loads = [
        (filt, filt_v), (key, key_v), (value, value_v),
        (head_in_h, head_in), (turn_h, turn), (tail_in_h, tail_in),
        (block_in_h, block_in), (block_out_h.at[me % 2], block_out),
        (tail_out_h, tail_out), (head_out_h, head_out), (query, query_v),
    ]
    loads = [pltpu.make_async_copy(a, b, load_sem.at[i]) for i, (a, b) in enumerate(loads)]
    for load in loads:
        load.start()
    (l_filt, l_key, l_value, l_hi, l_turn, l_ti, l_bi, l_bo, l_to, l_ho, l_query) = loads

    barrier = pltpu.get_barrier_semaphore()

    @pl.loop(1, 8)
    def _(i):
        pl.semaphore_signal(barrier, inc=1, device_id=z_device((z + i) % 8), device_id_type=MESH)

    pl.semaphore_signal(
        barrier, inc=1, device_id={"seq": (seq + 127) % 128, "ch": ch}, device_id_type=MESH
    )

    @pl.loop(1, 32)
    def _(i):
        pl.semaphore_signal(barrier, inc=1, device_id=xy_device((me + i) % 32), device_id_type=MESH)

    pl.semaphore_wait(barrier, 39)

    halos = [
        pltpu.make_async_remote_copy(
            src_ref=source.at[:, 8064:8192],
            dst_ref=halo.at[i],
            send_sem=halo_send.at[i],
            recv_sem=halo_recv.at[i],
            device_id={"seq": (seq + 1) % 128, "ch": ch},
            device_id_type=MESH,
        )
        for i, source in enumerate((key, value))
    ]
    for copy in halos:
        copy.start()

    def z_exchange(f):
        @pl.loop(1, 4)
        def _(i):
            to = (zh + i) % 4
            pltpu.make_async_remote_copy(
                src_ref=rows.at[f, to],
                dst_ref=zbuf.at[f, zh],
                send_sem=z_send.at[f],
                recv_sem=z_recv.at[f],
                device_id=z_device(to * 2 + ch),
                device_id_type=MESH,
            ).start()

        pltpu.make_async_copy(rows.at[f, zh], zbuf.at[f, zh], z_recv.at[f]).start()

    l_filt.wait()
    rows[0] = filt_v[...].reshape(4, 64, 128)
    first = jnp.where((lax.broadcasted_iota(jnp.int32, (1, 128), 1) == 0) & (seq == 0), 1.0, 0.0)
    for c in range(4):
        rows[0, c, 0:1, :] = rows[0, c, 0:1, :] + first * bias[c]
    z_exchange(0)

    l_key.wait()
    l_value.wait()

    def short(source, i):
        x = source[...]
        t = taps[i]
        return t[:, 0:1] * x + t[:, 1:2] * pltpu.roll(x, 1, 1) + t[:, 2:3] * pltpu.roll(x, 2, 1)

    rows[1] = (short(key_v, 0) * short(value_v, 1)).reshape(4, 64, 128)
    for copy in halos:
        copy.wait_recv()
    lane = lax.broadcasted_iota(jnp.int32, (4, 128), 1)

    def short_first(source, i):
        x = source[:, 0:128]
        t = taps[i]
        before = jnp.where(seq > 0, halo[i], 0.0)
        x1 = jnp.where(lane < 1, pltpu.roll(before, 1, 1), pltpu.roll(x, 1, 1))
        x2 = jnp.where(lane < 2, pltpu.roll(before, 2, 1), pltpu.roll(x, 2, 1))
        return t[:, 0:1] * x + t[:, 1:2] * x1 + t[:, 2:3] * x2

    fixed = short_first(key_v, 0) * short_first(value_v, 1)
    for c in range(4):
        rows[1, c, 0:1, :] = fixed[c : c + 1, :]
    z_exchange(1)

    def forward(f):
        pltpu.make_async_copy(zbuf.at[f], zbuf.at[f], z_recv.at[f]).wait()
        put_split(right_a, zbuf[f].reshape(256, 128), 0)
        if f == 0:
            l_hi.wait()
        real = mm(head_in[0:256, :], right_a[...])
        imag = mm(head_in[256:512, :], right_a[...])
        if f == 0:
            l_turn.wait()
            l_ti.wait()
        c, sn = turn[:, 0:128], turn[:, 128:256]
        turned = jnp.concatenate([real * c + imag * sn, imag * c - real * sn], axis=1)
        put_split(left_b, turned, 1)
        sbuf[f] = mm(left_b[...], tail_in[...]).reshape(32, 8, 256)

        @pl.loop(1, 32)
        def _(i):
            d = (me + i) % 32
            pltpu.make_async_remote_copy(
                src_ref=sbuf.at[f, d],
                dst_ref=rbuf.at[f, me],
                send_sem=xy_send.at[f],
                recv_sem=xy_recv.at[f],
                device_id=xy_device(d),
                device_id_type=MESH,
            ).start()

        pltpu.make_async_copy(sbuf.at[f, me], rbuf.at[f, me], xy_recv.at[f]).start()

    def across(f):
        pltpu.make_async_copy(rbuf.at[f], rbuf.at[f], xy_recv.at[f]).wait()
        put_split(right_q, rbuf[f].reshape(256, 256), 0)
        if f == 0:
            l_bi.wait()
        for m in range(0, 512, 128):
            cosines = mm(block_in[m : m + 128, :], right_q[...])
            sines = mm(block_in[512 + m : 640 + m, :], right_q[...])
            real = cosines[:, 0:128] + sines[:, 128:256]
            imag = cosines[:, 128:256] - sines[:, 0:128]
            if f == 0:
                spec[m : m + 128, 0:128] = real
                spec[m : m + 128, 128:256] = imag
            else:
                freal, fimag = spec[m : m + 128, 0:128], spec[m : m + 128, 128:256]
                prod = jnp.concatenate([real * freal - imag * fimag, real * fimag + imag * freal], axis=1)
                high = prod.astype(BF16)
                low = (prod - high.astype(F32)).astype(BF16)
                right_i[m : m + 128, :] = high
                right_i[512 + m : 640 + m, :] = low
                right_i[1024 + m : 1152 + m, :] = high

    forward(0)
    forward(1)
    across(0)
    across(1)
    l_bo.wait()
    for m in range(0, 256, 128):
        cosines = mm(block_out[m : m + 128, :], right_i[...])
        sines = mm(block_out[256 + m : 384 + m, :], right_i[...])
        real = cosines[:, 0:128] - sines[:, 128:256]
        imag = cosines[:, 128:256] + sines[:, 0:128]
        back_s[m // 8 : m // 8 + 16] = jnp.concatenate([real, imag], axis=1).reshape(16, 8, 256)

    @pl.loop(1, 32)
    def _(i):
        d = (me + i) % 32
        pltpu.make_async_remote_copy(
            src_ref=back_s.at[d],
            dst_ref=back_r.at[me],
            send_sem=back_send,
            recv_sem=back_recv,
            device_id=xy_device(d),
            device_id_type=MESH,
        ).start()

    pltpu.make_async_copy(back_s.at[me], back_r.at[me], back_recv).start()
    pltpu.make_async_copy(back_r, back_r, back_recv).wait()

    put_split(left_o, back_r[...].reshape(256, 256), 1)
    l_to.wait()
    mixed = mm(left_o[...], tail_out[...])
    c, sn = turn[:, 0:128], turn[:, 128:256]
    real, imag = mixed[:, 0:128], mixed[:, 128:256]
    put_split(right_o, jnp.concatenate([real * c - imag * sn, real * sn + imag * c], axis=0), 0)
    l_ho.wait()
    done_s[...] = mm(head_out[...], right_o[...]).reshape(8, 32, 128)

    channel = ch * 4 + zh

    @pl.loop(1, 8)
    def _(i):
        to = (z + i) % 8
        pltpu.make_async_remote_copy(
            src_ref=done_s.at[to],
            dst_ref=done_r.at[channel],
            send_sem=done_send,
            recv_sem=done_recv,
            device_id=z_device(to),
            device_id_type=MESH,
        ).start()

    pltpu.make_async_copy(done_s.at[z], done_r.at[channel], done_recv).start()
    l_query.wait()
    pltpu.make_async_copy(done_r, done_r, done_recv).wait()
    out[...] = done_r[...].reshape(8, 4096) * query_v[...]

    for copy in halos:
        copy.wait_send()
    for f in range(2):
        pltpu.make_async_copy(rows.at[f, 0:3], rows.at[f, 0:3], z_send.at[f]).wait()
        pltpu.make_async_copy(sbuf.at[f, 0:31], sbuf.at[f, 0:31], xy_send.at[f]).wait()
    pltpu.make_async_copy(back_s.at[0:31], back_s.at[0:31], back_send).wait()
    pltpu.make_async_copy(done_s.at[0:7], done_s.at[0:7], done_send).wait()


def local(query, key, value, filters, short_taps, bias):
    tables = make_tables()
    vm = pltpu.VMEM
    dma = pltpu.SemaphoreType.DMA
    any_spec = pl.BlockSpec(memory_space=pl.ANY)
    table_scratch = [vm(t.shape[1:] if t.ndim == 3 else t.shape, t.dtype) for t in tables]
    return pl.pallas_call(
        kernel,
        out_shape=jax.ShapeDtypeStruct((8, 4096), F32),
        in_specs=[
            pl.BlockSpec(memory_space=pltpu.VMEM),
            pl.BlockSpec(memory_space=pltpu.SMEM),
        ]
        + [any_spec] * 11,
        out_specs=pl.BlockSpec(memory_space=pltpu.VMEM),
        scratch_shapes=[vm((8, 4096), F32)]
        + [vm((4, 8192), F32)] * 3
        + table_scratch
        + [
            vm((2, 4, 128), F32),
            vm((2, 4, 64, 128), F32),
            vm((2, 4, 64, 128), F32),
            vm((2, 32, 8, 256), F32),
            vm((2, 32, 8, 256), F32),
            vm((512, 256), F32),
            vm((8, 128), F32),
            vm((32, 8, 256), F32),
            vm((32, 8, 256), F32),
            vm((8, 32, 128), F32),
            vm((8, 32, 128), F32),
            vm((768, 128), BF16),
            vm((256, 768), BF16),
            vm((768, 256), BF16),
            vm((1536, 256), BF16),
            vm((256, 768), BF16),
            vm((1536, 128), BF16),
            dma((11,)),
            dma((2,)), dma((2,)),
            dma((2,)), dma((2,)),
            dma((2,)), dma((2,)),
            dma(()), dma(()),
            dma(()), dma(()),
        ],
        compiler_params=pltpu.CompilerParams(
            collective_id=0, has_side_effects=True, vmem_limit_bytes=56 * 1024 * 1024
        ),
        name="long_convolution",
    )(short_taps, bias, query, key, value, filters, *[jnp.asarray(t) for t in tables])


def solution(mesh):
    return jax.shard_map(
        local,
        mesh=mesh,
        in_specs=(
            P(None, ("seq", "ch")),
            P("ch", "seq"),
            P("ch", "seq"),
            P("ch", "seq"),
            P(None, "ch", None),
            P("ch"),
        ),
        out_specs=P(None, ("seq", "ch")),
        check_vma=False,
    )
```

```python
import functools

import jax
import jax.numpy as jnp
import ml_dtypes
import numpy as np
from jax import lax
from jax.experimental import pallas as pl
from jax.experimental.pallas import tpu as pltpu
from jax.sharding import PartitionSpec as P

MESH = pl.DeviceIdType.MESH
F32 = jnp.float32
BF16 = jnp.bfloat16


def two_parts(table):
    high = table.astype(np.float32).astype(ml_dtypes.bfloat16)
    low = (table - high.astype(np.float64)).astype(np.float32).astype(ml_dtypes.bfloat16)
    return high, low


def as_left(table):
    high, low = two_parts(table)
    return np.concatenate([high, high, low], axis=1)


def as_right(table):
    high, low = two_parts(table)
    return np.concatenate([high, high, low], axis=0)


def make_tables():
    j1, k1 = np.arange(32), np.arange(32)
    lanes = np.arange(128)
    head = 2 * np.pi * np.outer(k1 + 0.5, j1) / 64
    same = np.eye(8)
    step = np.stack([np.cos(head), -np.sin(head)])
    head_in = np.einsum("rkj,ab->rkabj", step, same).reshape(512, 256)
    head_out = np.einsum("rkj,ab->bjrka", step, same).reshape(256, 512)
    turn = np.repeat(2 * np.pi * np.outer(k1 + 0.5, lanes) / 8192, 8, axis=0)
    turn = np.concatenate([np.cos(turn), np.sin(turn)], axis=1).astype(np.float32)
    tail = 2 * np.pi * np.outer(lanes, lanes) / 128
    c, s = np.cos(tail), np.sin(tail)
    tail_in = np.block([[c, -s], [s, c]])
    tail_out = np.block([[c, s], [-s, c]])
    place = np.arange(256).reshape(4, 4, 8, 2).transpose(0, 2, 1, 3).reshape(256)
    nu = np.arange(512)
    phase = 2 * np.pi * np.outer(nu, place) / 512
    block_in = np.concatenate([np.cos(phase), np.sin(phase)], axis=0)
    block_out = []
    for sign in (1, -1):
        wave = np.exp(1j * phase.T) * (1 + sign * 1j * np.exp(-2j * np.pi * nu / 512))[None, :]
        wave = wave * 2.0**-21
        block_out.append(as_left(np.concatenate([wave.real, wave.imag], axis=0)))
    return (
        as_left(head_in),
        as_right(tail_in),
        turn,
        as_left(block_in),
        np.stack(block_out),
        as_right(tail_out),
        as_left(head_out),
    )


def put_split(ref, value, axis):
    high = value.astype(BF16)
    low = (value - high.astype(F32)).astype(BF16)
    n = value.shape[axis]
    for place, part in enumerate((high, low, high)):
        if axis == 0:
            ref[place * n : (place + 1) * n, :] = part
        else:
            ref[:, place * n : (place + 1) * n] = part


def mm(a, b):
    return jnp.dot(a, b, preferred_element_type=F32)


def kernel(
    key, value, filt, taps_h, bias_h,
    head_in_h, tail_in_h, turn_h, block_in_h, block_out_h, tail_out_h, head_out_h,
    out,
    key_v, value_v, filt_v, taps, bias,
    head_in, tail_in, turn, block_in, block_out, tail_out, head_out,
    gate, ends_s, ends_r, rows_f, rows_s, zbuf_f, zbuf_s, sbuf, rbuf, spec, back_s, back_r, done_s, done_r,
    right_a, left_b, right_q, right_i, left_o, right_o,
    load_sem, ends_send, ends_recv, z_send, z_recv, xy_send, xy_recv,
    back_send, back_recv, done_send, done_recv,
):
    seq = lax.axis_index("seq")
    ch = lax.axis_index("ch")
    y = seq // 32
    zh = (seq // 8) % 4
    s = seq % 8
    me = y * 8 + s
    z = zh * 2 + ch

    def xy_device(d):
        return {"seq": (d // 8) * 32 + zh * 8 + d % 8, "ch": ch}

    def z_device(to):
        return {"seq": y * 32 + (to // 2) * 8 + s, "ch": to % 2}

    barrier = pltpu.get_barrier_semaphore()

    @pl.loop(0, 7)
    def _(i):
        pl.semaphore_signal(
            barrier, inc=1, device_id=z_device((z + 1 + (i + 3) % 7) % 8), device_id_type=MESH
        )

    @pl.loop(0, 4)
    def _(i):
        before = (y * 32 + i * 8 + s + 127) % 128
        pl.semaphore_signal(barrier, inc=1, device_id={"seq": before, "ch": ch}, device_id_type=MESH)

    @pl.loop(1, 32)
    def _(i):
        pl.semaphore_signal(barrier, inc=1, device_id=xy_device((me + i) % 32), device_id_type=MESH)

    loads = [
        (filt, filt_v), (bias_h, bias), (key, key_v), (value, value_v), (taps_h, taps),
        (head_in_h, head_in), (turn_h, turn), (tail_in_h, tail_in),
        (block_in_h, block_in), (block_out_h.at[me % 2], block_out),
        (tail_out_h, tail_out), (head_out_h, head_out),
    ]
    loads = [pltpu.make_async_copy(a, b, load_sem.at[i]) for i, (a, b) in enumerate(loads)]
    for load in loads:
        load.start()
    drains = []
    pend = {}
    (l_filt, l_bias, l_key, l_value, l_taps, l_hi, l_turn, l_ti, l_bi, l_bo, l_to, l_ho) = loads

    l_filt.wait()
    l_bias.wait()
    for c in range(4):
        rows_f[c] = filt_v[pl.ds(c, 64, stride=4), :]
    first = jnp.where((lax.broadcasted_iota(jnp.int32, (1, 128), 1) == 0) & (seq == 0), 1.0, 0.0)
    for c in range(4):
        rows_f[c, 0:1, :] = rows_f[c, 0:1, :] + first * bias[c]

    l_key.wait()
    l_value.wait()
    l_taps.wait()
    for c in range(4):
        for i, source in enumerate((key_v, value_v)):
            rows_s[c, 64 + i : 65 + i, :] = source[c : c + 1, :]
            ends_s[c, i : i + 1, :] = source[252 + c : 253 + c, :]

    pl.semaphore_wait(barrier, 42)
    zbuf = (zbuf_f, zbuf_s)
    rows = (rows_f, rows_s)

    def z_exchange(f):
        @pl.loop(1, 4)
        def _(i):
            to = (zh + 1 + i % 3) % 4
            pltpu.make_async_remote_copy(
                src_ref=rows[f].at[to],
                dst_ref=zbuf[f].at[zh],
                send_sem=z_send.at[f],
                recv_sem=z_recv.at[f],
                device_id=z_device(to * 2 + ch),
                device_id_type=MESH,
            ).start()

        pltpu.make_async_copy(rows[f].at[zh], zbuf[f].at[zh], z_recv.at[f]).start()
        pend['z',f] = pltpu.make_async_copy(zbuf[f], zbuf[f], z_recv.at[f])
        drains.append(lambda: pltpu.make_async_copy(rows[f].at[0:3], rows[f].at[0:3], z_send.at[f]).wait())

    z_exchange(0)

    after = (seq + 1) % 128

    @pl.loop(0, 4)
    def _(c):
        pltpu.make_async_remote_copy(
            src_ref=ends_s.at[c],
            dst_ref=ends_r.at[(after // 8) % 4],
            send_sem=ends_send,
            recv_sem=ends_recv,
            device_id={"seq": (after // 32) * 32 + c * 8 + after % 8, "ch": ch},
            device_id_type=MESH,
        ).start()

    pend['e'] = pltpu.make_async_copy(ends_r, ends_r, ends_recv)
    drains.append(lambda: pltpu.make_async_copy(ends_s, ends_s, ends_send).wait())

    row = lax.broadcasted_iota(jnp.int32, (8, 128), 0) % 4
    lanes = lax.broadcasted_iota(jnp.int32, (256, 128), 1)

    def short(source, i):
        x = source[...]
        total = None
        for j in range(3):
            t = [taps[j, i, c] for c in range(4)]
            t = jnp.where(row < 2, jnp.where(row == 0, t[0], t[1]), jnp.where(row == 2, t[2], t[3]))
            moved = x
            if j > 0:
                near = pltpu.roll(x, j, 1)
                moved = jnp.where(lanes < j, pltpu.roll(near, 4, 0), near)
            term = t[None] * moved.reshape(32, 8, 128)
            total = term if total is None else total + term
        return total

    gate[...] = (short(key_v, 0) * short(value_v, 1)).reshape(256, 128)
    for c in range(4):
        rows_s[c, 0:64, :] = gate[pl.ds(c, 64, stride=4), :]
    z_exchange(1)

    def first_rows():
        pend.pop('e').wait()
        lane = lax.broadcasted_iota(jnp.int32, (4, 128), 1)
        origin = lax.broadcasted_iota(jnp.int32, (4, 128), 0) + me == 0

        def whole(i):
            x = zbuf_s[:, 64 + i, :]
            before = jnp.where(origin, 0.0, ends_r[:, i, :])
            total = taps[0, i, zh] * x
            for j in (1, 2):
                moved = jnp.where(lane < j, pltpu.roll(before, j, 1), pltpu.roll(x, j, 1))
                total = total + taps[j, i, zh] * moved
            return total

        fixed = whole(0) * whole(1)
        for block in range(4):
            zbuf_s[block, 0:1, :] = fixed[block : block + 1, :]

    def forward(f):
        pend.pop(('z',f)).wait()
        if f == 1:
            first_rows()
        put_split(right_a, zbuf[f][:, 0:64, :].reshape(256, 128), 0)
        if f == 0:
            l_hi.wait()
        real = mm(head_in[0:256, :], right_a[...])
        imag = mm(head_in[256:512, :], right_a[...])
        if f == 0:
            l_turn.wait()
            l_ti.wait()
        c, sn = turn[:, 0:128], turn[:, 128:256]
        turned = jnp.concatenate([real * c + imag * sn, imag * c - real * sn], axis=1)
        put_split(left_b, turned, 1)
        sbuf[f] = mm(left_b[...], tail_in[...]).reshape(32, 8, 256)

        @pl.loop(1, 32)
        def _(i):
            d = (me + i) % 32
            pltpu.make_async_remote_copy(
                src_ref=sbuf.at[f, d],
                dst_ref=rbuf.at[f, me],
                send_sem=xy_send.at[f],
                recv_sem=xy_recv.at[f],
                device_id=xy_device(d),
                device_id_type=MESH,
            ).start()

        pltpu.make_async_copy(sbuf.at[f, me], rbuf.at[f, me], xy_recv.at[f]).start()
        pend['x',f] = pltpu.make_async_copy(rbuf.at[f], rbuf.at[f], xy_recv.at[f])
        drains.append(lambda: pltpu.make_async_copy(sbuf.at[f, 0:31], sbuf.at[f, 0:31], xy_send.at[f]).wait())

    def across(f):
        pend.pop(('x',f)).wait()
        put_split(right_q, rbuf[f].reshape(256, 256), 0)
        if f == 0:
            l_bi.wait()
        for m in range(0, 512, 128):
            cosines = mm(block_in[m : m + 128, :], right_q[...])
            sines = mm(block_in[512 + m : 640 + m, :], right_q[...])
            real = cosines[:, 0:128] + sines[:, 128:256]
            imag = cosines[:, 128:256] - sines[:, 0:128]
            if f == 0:
                spec[m : m + 128, 0:128] = real
                spec[m : m + 128, 128:256] = imag
            else:
                freal, fimag = spec[m : m + 128, 0:128], spec[m : m + 128, 128:256]
                prod = jnp.concatenate([real * freal - imag * fimag, real * fimag + imag * freal], axis=1)
                high = prod.astype(BF16)
                low = (prod - high.astype(F32)).astype(BF16)
                right_i[m : m + 128, :] = high
                right_i[512 + m : 640 + m, :] = low
                right_i[1024 + m : 1152 + m, :] = high

    forward(0)
    forward(1)
    across(0)
    across(1)
    l_bo.wait()
    for m in range(0, 256, 128):
        cosines = mm(block_out[m : m + 128, :], right_i[...])
        sines = mm(block_out[256 + m : 384 + m, :], right_i[...])
        real = cosines[:, 0:128] - sines[:, 128:256]
        imag = cosines[:, 128:256] + sines[:, 0:128]
        back_s[m // 8 : m // 8 + 16] = jnp.concatenate([real, imag], axis=1).reshape(16, 8, 256)

    @pl.loop(1, 32)
    def _(i):
        d = (me + i) % 32
        pltpu.make_async_remote_copy(
            src_ref=back_s.at[d],
            dst_ref=back_r.at[me],
            send_sem=back_send,
            recv_sem=back_recv,
            device_id=xy_device(d),
            device_id_type=MESH,
        ).start()

    pltpu.make_async_copy(back_s.at[me], back_r.at[me], back_recv).start()
    drains.append(lambda: pltpu.make_async_copy(back_s.at[0:31], back_s.at[0:31], back_send).wait())
    pltpu.make_async_copy(back_r, back_r, back_recv).wait()

    put_split(left_o, back_r[...].reshape(256, 256), 1)
    l_to.wait()
    mixed = mm(left_o[...], tail_out[...])
    c, sn = turn[:, 0:128], turn[:, 128:256]
    real, imag = mixed[:, 0:128], mixed[:, 128:256]
    put_split(right_o, jnp.concatenate([real * c - imag * sn, real * sn + imag * c], axis=0), 0)
    l_ho.wait()
    done_s[...] = mm(head_out[...], right_o[...])

    channel = ch * 4 + zh

    @pl.loop(1, 8)
    def _(i):
        to = (z + i) % 8
        pltpu.make_async_remote_copy(
            src_ref=done_s.at[pl.ds(pl.multiple_of(to * 32, 32), 32)],
            dst_ref=done_r.at[pl.ds(pl.multiple_of(channel * 32, 32), 32)],
            send_sem=done_send,
            recv_sem=done_recv,
            device_id=z_device(to),
            device_id_type=MESH,
        ).start()

    pltpu.make_async_copy(
        done_s.at[pl.ds(pl.multiple_of(z * 32, 32), 32)],
        done_r.at[pl.ds(pl.multiple_of(channel * 32, 32), 32)],
        done_recv,
    ).start()
    drains.append(lambda: pltpu.make_async_copy(done_s.at[0:224], done_s.at[0:224], done_send).wait())
    pltpu.make_async_copy(done_r, done_r, done_recv).wait()
    for j in range(32):
        out[8 * j : 8 * j + 8, :] = done_r[pl.ds(j, 8, stride=32), :]

    for drain in drains:
        drain()


def by_time(x):
    return x.reshape(4, 64, 128).transpose(1, 0, 2).reshape(256, 128)


def local(query, key, value, filters, short_taps, bias):
    tables = make_tables()
    vm = pltpu.VMEM
    dma = pltpu.SemaphoreType.DMA
    table_scratch = [vm(t.shape[1:] if t.ndim == 3 else t.shape, t.dtype) for t in tables]
    conv = pl.pallas_call(
        kernel,
        out_shape=jax.ShapeDtypeStruct((256, 128), F32),
        in_specs=[pl.BlockSpec(memory_space=pl.ANY)] * 12,
        out_specs=pl.BlockSpec(memory_space=pltpu.VMEM),
        scratch_shapes=[vm((256, 128), F32)] * 3
        + [pltpu.SMEM((3, 2, 4), F32), pltpu.SMEM((4,), F32)]
        + table_scratch
        + [
            vm((256, 128), F32),
            vm((4, 8, 128), F32),
            vm((4, 8, 128), F32),
            vm((4, 64, 128), F32),
            vm((4, 72, 128), F32),
            vm((4, 64, 128), F32),
            vm((4, 72, 128), F32),
            vm((2, 32, 8, 256), F32),
            vm((2, 32, 8, 256), F32),
            vm((512, 256), F32),
            vm((32, 8, 256), F32),
            vm((32, 8, 256), F32),
            vm((256, 128), F32),
            vm((256, 128), F32),
            vm((768, 128), BF16),
            vm((256, 768), BF16),
            vm((768, 256), BF16),
            vm((1536, 256), BF16),
            vm((256, 768), BF16),
            vm((1536, 128), BF16),
            dma((12,)),
            dma(()), dma(()),
            dma((2,)), dma((2,)),
            dma((2,)), dma((2,)),
            dma(()), dma(()),
            dma(()), dma(()),
        ],
        compiler_params=pltpu.CompilerParams(
            collective_id=0, has_side_effects=True, vmem_limit_bytes=56 * 1024 * 1024
        ),
        name="long_convolution",
    )(
        by_time(key), by_time(value), by_time(filters), short_taps.transpose(2, 0, 1), bias,
        *[jnp.asarray(t) for t in tables],
    )
    return conv.reshape(32, 8, 128).transpose(1, 0, 2).reshape(8, 4096) * query


def solution(mesh):
    return jax.shard_map(
        local,
        mesh=mesh,
        in_specs=(
            P(None, ("seq", "ch")),
            P("ch", "seq"),
            P("ch", "seq"),
            P("ch", "seq"),
            P(None, "ch", None),
            P("ch"),
        ),
        out_specs=P(None, ("seq", "ch")),
        check_vma=False,
    )
```

```python
import functools

import jax
import jax.numpy as jnp
import ml_dtypes
import numpy as np
from jax import lax
from jax.experimental import pallas as pl
from jax.experimental.pallas import tpu as pltpu
from jax.sharding import PartitionSpec as P

MESH = pl.DeviceIdType.MESH
F32 = jnp.float32
BF16 = jnp.bfloat16


def two_parts(table):
    high = table.astype(np.float32).astype(ml_dtypes.bfloat16)
    low = (table - high.astype(np.float64)).astype(np.float32).astype(ml_dtypes.bfloat16)
    return high, low


def as_left(table):
    high, low = two_parts(table)
    return np.concatenate([high, high, low], axis=1)


def as_right(table):
    high, low = two_parts(table)
    return np.concatenate([high, high, low], axis=0)


FORWARD = ((0, 1), (3, 2))
BACK = ((0, 1, 2, 3), (4, 5, 6, 7))


def make_tables():
    j1, k1 = np.arange(32), np.arange(32)
    lanes = np.arange(128)
    head = 2 * np.pi * np.outer(k1 + 0.5, j1) / 64
    same = np.eye(4)
    step = np.stack([np.cos(head), -np.sin(head)])
    head_in = np.einsum("rkj,ab->rkabj", step, same).reshape(256, 128)
    head_out = np.einsum("rkj,ab->bjrka", step, same).reshape(128, 256)
    turn = np.repeat(2 * np.pi * np.outer(k1 + 0.5, lanes) / 8192, 4, axis=0)
    turn = np.concatenate([np.cos(turn), np.sin(turn)], axis=1).astype(np.float32)
    tail = 2 * np.pi * np.outer(lanes, lanes) / 128
    c, s = np.cos(tail), np.sin(tail)
    tail_in = np.block([[c, -s], [s, c]])
    tail_out = np.block([[c, s], [-s, c]])
    place = np.arange(256).reshape(4, 4, 8, 2).transpose(1, 3, 0, 2).reshape(256)
    nu = np.arange(512)
    phase = 2 * np.pi * np.outer(nu, place) / 512
    block_in = np.concatenate([np.cos(phase), np.sin(phase)], axis=0)
    block_out = []
    for sign in (1, -1):
        wave = np.exp(1j * phase.T) * (1 + sign * 1j * np.exp(-2j * np.pi * nu / 512))[None, :]
        wave = wave.reshape(8, 32, 512) * 2.0**-21
        wave = np.stack([wave.real, wave.imag], axis=1).reshape(512, 512)
        block_out.append(as_left(wave))
    return (
        as_left(head_in),
        as_right(tail_in),
        turn,
        as_left(block_in),
        np.stack(block_out),
        as_right(tail_out),
        as_left(head_out),
    )


def put_split(ref, value, axis):
    high = value.astype(BF16)
    low = (value - high.astype(F32)).astype(BF16)
    n = value.shape[axis]
    for place, part in enumerate((high, low, high)):
        if axis == 0:
            ref[place * n : (place + 1) * n, :] = part
        else:
            ref[:, place * n : (place + 1) * n] = part


def mm(a, b):
    return jnp.dot(a, b, preferred_element_type=F32)


def kernel(
    key, value, filt, taps_h, bias_h,
    head_in_h, tail_in_h, turn_h, block_in_h, block_out_h, tail_out_h, head_out_h,
    out,
    key_v, value_v, filt_v, taps, bias,
    head_in, tail_in, turn, block_in, block_out, tail_out, head_out,
    gate, ends_s, ends_z, ends_r, starts, rows_f, rows_s, zbuf_f, zbuf_s, sbuf, rbuf, spec, back_s, back_r, done_s, done_r,
    right_a, left_b, right_q, right_i, left_o, right_o,
    load_sem, ends_send, ends_recv, z_send, z_recv, xy_send, xy_recv,
    back_send, back_recv, done_send, done_recv,
):
    seq = lax.axis_index("seq")
    ch = lax.axis_index("ch")
    y = seq // 32
    zh = (seq // 8) % 4
    s = seq % 8
    me = y * 8 + s
    z = zh * 2 + ch
    zbuf = (zbuf_f, zbuf_s)
    rows = (rows_f, rows_s)

    def xy_device(d):
        return {"seq": (d // 8) * 32 + zh * 8 + d % 8, "ch": ch}

    def z_device(to):
        return {"seq": y * 32 + (to // 2) * 8 + s, "ch": to % 2}

    def tile(i, n=8):
        return pl.ds(pl.multiple_of(i * n, n), n)

    def total(ref, sem):
        return pltpu.make_async_copy(ref, ref, sem)

    barrier = pltpu.get_barrier_semaphore()

    @pl.loop(0, 7)
    def _(i):
        pl.semaphore_signal(
            barrier, inc=1, device_id=z_device((z + 1 + (i + 3) % 7) % 8), device_id_type=MESH
        )

    @pl.loop(1, 32)
    def _(i):
        pl.semaphore_signal(barrier, inc=1, device_id=xy_device((me + i) % 32), device_id_type=MESH)

    loads = [
        (filt, filt_v), (bias_h, bias), (key, key_v), (value, value_v), (taps_h, taps),
        (head_in_h, head_in), (turn_h, turn), (tail_in_h, tail_in),
        (block_in_h, block_in), (block_out_h.at[me % 2], block_out),
        (tail_out_h, tail_out), (head_out_h, head_out),
    ]
    loads = [pltpu.make_async_copy(a, b, load_sem.at[i]) for i, (a, b) in enumerate(loads)]
    for load in loads:
        load.start()
    drains = []
    pend = {}
    (l_filt, l_bias, l_key, l_value, l_taps, l_hi, l_turn, l_ti, l_bi, l_bo, l_to, l_ho) = loads

    l_filt.wait()
    l_bias.wait()
    for c in range(4):
        rows_f[c] = filt_v[pl.ds(c, 64, stride=4), :]
    first = jnp.where((lax.broadcasted_iota(jnp.int32, (1, 128), 1) == 0) & (seq == 0), 1.0, 0.0)
    for c in range(4):
        rows_f[c, 0:1, :] = rows_f[c, 0:1, :] + first * bias[c]

    l_key.wait()
    l_value.wait()
    l_taps.wait()
    for i, source in enumerate((key_v, value_v)):
        for c in range(4):
            ends_s[c, i : i + 1, :] = source[252 + c : 253 + c, :]
            ends_s[c, 2 + i : 3 + i, :] = source[c : c + 1, :]
    row = lax.broadcasted_iota(jnp.int32, (8, 128), 0) % 4
    lanes = lax.broadcasted_iota(jnp.int32, (256, 128), 1)

    def tap_rows(j, i):
        t = [taps[j, i, c] for c in range(4)]
        return jnp.where(row < 2, jnp.where(row == 0, t[0], t[1]), jnp.where(row == 2, t[2], t[3]))

    def short(source, i):
        x = source[...]
        result = None
        for j in range(3):
            t = tap_rows(j, i)
            moved = x
            if j > 0:
                near = pltpu.roll(x, j, 1)
                moved = jnp.where(lanes < j, pltpu.roll(near, 4, 0), near)
            term = t[None] * moved.reshape(32, 8, 128)
            result = term if result is None else result + term
        return result

    gate[...] = (short(key_v, 0) * short(value_v, 1)).reshape(256, 128)
    for c in range(4):
        rows_s[c] = gate[pl.ds(c, 64, stride=4), :]

    pl.semaphore_wait(barrier, 38)

    for i in (2, 3, 1):
        to = (zh + i) % 4
        pltpu.make_async_remote_copy(
            src_ref=ends_s.at[to],
            dst_ref=ends_z.at[zh],
            send_sem=ends_send.at[0],
            recv_sem=ends_recv.at[0],
            device_id=z_device(to * 2 + ch),
            device_id_type=MESH,
        ).start()
    drains.append(total(ends_s.at[0:3], ends_send.at[0]).wait)

    def z_exchange(f):
        for i in (2, 3, 1):
            to = (zh + i) % 4
            pltpu.make_async_remote_copy(
                src_ref=rows[f].at[to],
                dst_ref=zbuf[f].at[4 - i],
                send_sem=z_send.at[f],
                recv_sem=z_recv.at[f, 4 - i],
                device_id=z_device(to * 2 + ch),
                device_id_type=MESH,
            ).start()
            pend['z',f,4-i] = total(zbuf[f].at[4 - i], z_recv.at[f, 4 - i])
        drains.append(lambda: total(rows[f].at[0:3], z_send.at[f]).wait())

    z_exchange(0)
    z_exchange(1)
    ends_z[zh] = ends_s[zh]
    total(ends_z.at[0:3], ends_recv.at[0]).wait()

    @pl.loop(0, 4)
    def _(block):
        after = (y * 32 + block * 8 + s + 1) % 128
        pltpu.make_async_remote_copy(
            src_ref=ends_z.at[block],
            dst_ref=ends_r.at[(after // 8) % 4],
            send_sem=ends_send.at[1],
            recv_sem=ends_recv.at[1],
            device_id={"seq": (after // 32) * 32 + zh * 8 + after % 8, "ch": ch},
            device_id_type=MESH,
        ).start()

    pend['e'] = total(ends_r, ends_recv.at[1])
    drains.append(total(ends_z, ends_send.at[1]).wait)

    def first_rows():
        pend.pop('e').wait()
        lane = lax.broadcasted_iota(jnp.int32, (4, 128), 1)
        origin = lax.broadcasted_iota(jnp.int32, (4, 128), 0) + me == 0

        def whole(i):
            x = jnp.concatenate([ends_z[b, 2 + i : 3 + i, :] for b in range(4)], axis=0)
            before = jnp.concatenate([ends_r[b, i : i + 1, :] for b in range(4)], axis=0)
            before = jnp.where(origin, 0.0, before)
            result = taps[0, i, zh] * x
            for j in (1, 2):
                moved = jnp.where(lane < j, pltpu.roll(before, j, 1), pltpu.roll(x, j, 1))
                result = result + taps[j, i, zh] * moved
            return result

        fixed = whole(0) * whole(1)
        for b in range(4):
            starts[b, 0:1, :] = fixed[b : b + 1, :]

    for f in range(2):
        zbuf[f][0] = rows[f][zh]

    def forward(f, p):
        for d in FORWARD[p]:
            if d != 0:
                pend.pop(('z',f,d)).wait()
        if f == 1:
            if p == 0:
                first_rows()
            for d in FORWARD[p]:
                zbuf_s[d, 0:1, :] = starts[(zh + d) % 4, 0:1, :]
        put_split(right_a, jnp.concatenate([zbuf[f][d] for d in FORWARD[p]], axis=0), 0)
        if f == 0 and p == 0:
            l_hi.wait()
        real = mm(head_in[0:128, :], right_a[...])
        imag = mm(head_in[128:256, :], right_a[...])
        if f == 0 and p == 0:
            l_turn.wait()
            l_ti.wait()
        c, sn = turn[:, 0:128], turn[:, 128:256]
        turned = jnp.concatenate([real * c + imag * sn, imag * c - real * sn], axis=1)
        put_split(left_b, turned, 1)
        spread = mm(left_b[...], tail_in[...])
        sbuf[f, p, pl.ds(0, 128, stride=2), :] = spread[:, 0:128]
        sbuf[f, p, pl.ds(1, 128, stride=2), :] = spread[:, 128:256]

        @pl.loop(1, 32)
        def _(i):
            d = (me + i) % 32
            pltpu.make_async_remote_copy(
                src_ref=sbuf.at[f, p, tile(d)],
                dst_ref=rbuf.at[f, p, tile(me)],
                send_sem=xy_send.at[f, p],
                recv_sem=xy_recv.at[f, p],
                device_id=xy_device(d),
                device_id_type=MESH,
            ).start()

        rbuf[f, p, tile(me), :] = sbuf[f, p, tile(me), :]
        pend['x',f,p] = total(rbuf.at[f, p, 0:248], xy_recv.at[f, p])
        drains.append(lambda: total(sbuf.at[f, p, 0:248], xy_send.at[f, p]).wait())

    def across(f):
        for p in range(2):
            pend.pop(('x',f,p)).wait()
            for n, d in enumerate(FORWARD[p]):
                for half in range(2):
                    at = n * 4 + half * 2
                    pair = [rbuf[f, p, pl.ds(at + i, 32, stride=8), :] for i in range(2)]
                    pair = jnp.concatenate(pair, axis=1)
                    high = pair.astype(BF16)
                    low = (pair - high.astype(F32)).astype(BF16)
                    base = (zh + d) % 4 * 64 + half * 32
                    for k, part in enumerate((high, low, high)):
                        right_q[pl.ds(pl.multiple_of(base + 256 * k, 32), 32), :] = part
        if f == 0:
            l_bi.wait()
        for m in range(0, 512, 128):
            cosines = mm(block_in[m : m + 128, :], right_q[...])
            sines = mm(block_in[512 + m : 640 + m, :], right_q[...])
            real = cosines[:, 0:128] + sines[:, 128:256]
            imag = cosines[:, 128:256] - sines[:, 0:128]
            if f == 0:
                spec[m : m + 128, 0:128] = real
                spec[m : m + 128, 128:256] = imag
            else:
                freal, fimag = spec[m : m + 128, 0:128], spec[m : m + 128, 128:256]
                prod = jnp.concatenate([real * freal - imag * fimag, real * fimag + imag * freal], axis=1)
                high = prod.astype(BF16)
                low = (prod - high.astype(F32)).astype(BF16)
                right_i[m : m + 128, :] = high
                right_i[512 + m : 640 + m, :] = low
                right_i[1024 + m : 1152 + m, :] = high

    forward(0, 0)
    forward(0, 1)
    forward(1, 0)
    forward(1, 1)
    across(0)
    across(1)
    l_bo.wait()

    def send_back(p):
        both = mm(block_out[256 * p : 256 * p + 256, :], right_i[...])
        for n in range(4):
            cosines, sines = both[64 * n : 64 * n + 32], both[64 * n + 32 : 64 * n + 64]
            real = cosines[:, 0:128] - sines[:, 128:256]
            imag = cosines[:, 128:256] + sines[:, 0:128]
            back_s[p, pl.ds(2 * n, 32, stride=8), :] = real
            back_s[p, pl.ds(2 * n + 1, 32, stride=8), :] = imag

        @pl.loop(1, 32)
        def _(i):
            d = (me + i) % 32
            pltpu.make_async_remote_copy(
                src_ref=back_s.at[p, tile(d)],
                dst_ref=back_r.at[p, tile(me)],
                send_sem=back_send.at[p],
                recv_sem=back_recv.at[p],
                device_id=xy_device(d),
                device_id_type=MESH,
            ).start()

        back_r[p, tile(me), :] = back_s[p, tile(me), :]
        pend['b',p] = total(back_r.at[p, 0:248], back_recv.at[p])
        drains.append(lambda: total(back_s.at[p, 0:248], back_send.at[p]).wait())

    send_back(0)
    send_back(1)
    channel = ch * 4 + zh

    def finish_blocks(p):
        pend.pop(('b',p)).wait()
        pair = [back_r[p, pl.ds(i, 128, stride=2), :] for i in range(2)]
        put_split(left_o, jnp.concatenate(pair, axis=1), 1)
        if p == 0:
            l_to.wait()
            l_ho.wait()
        mixed = mm(left_o[...], tail_out[...])
        c, sn = turn[:, 0:128], turn[:, 128:256]
        real, imag = mixed[:, 0:128], mixed[:, 128:256]
        put_split(right_o, jnp.concatenate([real * c - imag * sn, real * sn + imag * c], axis=0), 0)
        done_s[128 * p : 128 * p + 128, :] = mm(head_out[...], right_o[...])

        @pl.loop(4 * p, 4 * p + 4)
        def _(to):
            @pl.when(to == z)
            def _():
                done_r[tile(channel, 32), :] = done_s[tile(to, 32), :]

            @pl.when(to != z)
            def _():
                pltpu.make_async_remote_copy(
                    src_ref=done_s.at[tile(to, 32)],
                    dst_ref=done_r.at[tile(channel, 32)],
                    send_sem=done_send,
                    recv_sem=done_recv,
                    device_id=z_device(to),
                    device_id_type=MESH,
                ).start()

    finish_blocks(0)
    finish_blocks(1)
    total(done_r.at[0:224], done_recv).wait()
    for j in range(32):
        out[8 * j : 8 * j + 8, :] = done_r[pl.ds(j, 8, stride=32), :]
    total(done_s.at[0:224], done_send).wait()
    for drain in drains:
        drain()


def by_time(x):
    return x.reshape(4, 64, 128).transpose(1, 0, 2).reshape(256, 128)


def local(query, key, value, filters, short_taps, bias):
    tables = make_tables()
    vm = pltpu.VMEM
    dma = pltpu.SemaphoreType.DMA
    table_scratch = [vm(t.shape if t.ndim == 2 else (512, 1536), t.dtype) for t in tables]
    conv = pl.pallas_call(
        kernel,
        out_shape=jax.ShapeDtypeStruct((256, 128), F32),
        in_specs=[pl.BlockSpec(memory_space=pl.ANY)] * 12,
        out_specs=pl.BlockSpec(memory_space=pltpu.VMEM),
        scratch_shapes=[vm((256, 128), F32)] * 3
        + [pltpu.SMEM((3, 2, 4), F32), pltpu.SMEM((4,), F32)]
        + table_scratch
        + [
            vm((256, 128), F32),
            vm((4, 8, 128), F32),
            vm((4, 8, 128), F32),
            vm((4, 8, 128), F32),
            vm((4, 8, 128), F32),
            vm((4, 64, 128), F32),
            vm((4, 64, 128), F32),
            vm((4, 64, 128), F32),
            vm((4, 64, 128), F32),
            vm((2, 2, 256, 128), F32),
            vm((2, 2, 256, 128), F32),
            vm((512, 256), F32),
            vm((2, 256, 128), F32),
            vm((2, 256, 128), F32),
            vm((256, 128), F32),
            vm((256, 128), F32),
            vm((384, 128), BF16),
            vm((128, 768), BF16),
            vm((768, 256), BF16),
            vm((1536, 256), BF16),
            vm((128, 768), BF16),
            vm((768, 128), BF16),
            dma((12,)),
            dma((2,)), dma((2,)),
            dma((2,)), dma((2, 4)),
            dma((2, 2)), dma((2, 2)),
            dma((2,)), dma((2,)),
            dma(()), dma(()),
        ],
        compiler_params=pltpu.CompilerParams(
            collective_id=0, has_side_effects=True, vmem_limit_bytes=56 * 1024 * 1024
        ),
        name="long_convolution",
    )(
        by_time(key), by_time(value), by_time(filters), short_taps.transpose(2, 0, 1), bias,
        *[jnp.asarray(t) for t in tables],
    )
    return conv.reshape(32, 8, 128).transpose(1, 0, 2).reshape(8, 4096) * query


def solution(mesh):
    return jax.shard_map(
        local,
        mesh=mesh,
        in_specs=(
            P(None, ("seq", "ch")),
            P("ch", "seq"),
            P("ch", "seq"),
            P("ch", "seq"),
            P(None, "ch", None),
            P("ch"),
        ),
        out_specs=P(None, ("seq", "ch")),
        check_vma=False,
    )
```

```python
import functools

import jax
import jax.numpy as jnp
import ml_dtypes
import numpy as np
from jax import lax
from jax.experimental import pallas as pl
from jax.experimental.pallas import tpu as pltpu
from jax.sharding import PartitionSpec as P

MESH = pl.DeviceIdType.MESH
F32 = jnp.float32
BF16 = jnp.bfloat16


def two_parts(table):
    high = table.astype(np.float32).astype(ml_dtypes.bfloat16)
    low = (table - high.astype(np.float64)).astype(np.float32).astype(ml_dtypes.bfloat16)
    return high, low


def as_left(table):
    high, low = two_parts(table)
    return np.concatenate([high, high, low], axis=1)


def as_right(table):
    high, low = two_parts(table)
    return np.concatenate([high, high, low], axis=0)


FORWARD = ((0, 1), (3, 2))
BACK = ((0, 1), (2, 3), (4, 5, 6, 7))
PLANE = sorted(
    ((a, b, e) for a in range(4) for b in range(4) for e in range(2) if (a, b, e) != (0, 0, 0)),
    key=lambda p: (-(2 - abs(2 - p[0])) - (2 - abs(2 - p[1])), p),
)


def make_tables():
    j1, k1 = np.arange(32), np.arange(32)
    lanes = np.arange(128)
    head = 2 * np.pi * np.outer(k1 + 0.5, j1) / 64
    step = np.stack([np.cos(head), -np.sin(head)])
    head_in = np.einsum("rkj,ab->rakbj", step, np.eye(4)).reshape(256, 128)
    head_out = [np.einsum("rkj,ab->bjrak", step, np.eye(n)).reshape(32 * n, 64 * n) for n in (2, 4)]
    angle = 2 * np.pi * np.outer(k1 + 0.5, lanes) / 8192
    turn = np.concatenate([np.cos(angle), np.sin(angle)], axis=1).astype(np.float32)
    turn = [np.tile(turn, (n, 1)) for n in (2, 4)]
    tail = 2 * np.pi * np.outer(lanes, lanes) / 128
    c, s = np.cos(tail), np.sin(tail)
    tail_in = np.block([[c, -s], [s, c]])
    tail_out = np.block([[c, s], [-s, c]])
    place = np.arange(256).reshape(4, 4, 8, 2).transpose(1, 3, 0, 2).reshape(256)
    nu = np.arange(512)
    phase = 2 * np.pi * np.outer(nu, place) / 512
    block_in = np.concatenate([np.cos(phase), np.sin(phase)], axis=0)
    block_out = []
    for sign in (1, -1):
        wave = np.exp(1j * phase.T) * (1 + sign * 1j * np.exp(-2j * np.pi * nu / 512))[None, :]
        wave = wave.reshape(8, 32, 512) * 2.0**-21
        wave = np.stack([wave.real, wave.imag], axis=1).reshape(512, 512)
        block_out.append(as_left(wave))
    return (
        as_left(head_in),
        as_right(tail_in),
        turn[0],
        turn[1],
        as_left(block_in),
        np.stack(block_out),
        as_right(tail_out),
        as_left(head_out[0]),
        as_left(head_out[1]),
    )


def put_split(ref, value, axis):
    high = value.astype(BF16)
    low = (value - high.astype(F32)).astype(BF16)
    n = value.shape[axis]
    for place, part in enumerate((high, low, high)):
        if axis == 0:
            ref[place * n : (place + 1) * n, :] = part
        else:
            ref[:, place * n : (place + 1) * n] = part


def mm(a, b):
    return jnp.dot(a, b, preferred_element_type=F32)


def kernel(
    key, value, filt, taps_h, bias_h,
    head_in_h, tail_in_h, turn2_h, turn4_h, block_in_h, block_out_h, tail_out_h, head_out2_h, head_out4_h,
    out,
    key_v, value_v, filt_v, taps, bias,
    head_in, tail_in, turn2, turn4, block_in, block_out, tail_out, head_out2, head_out4,
    gate, ends_s, ends_z, ends_r, starts, rows_f, rows_s, zbuf_f, zbuf_s, sbuf, rbuf, spec, back_s, back_r, done_s, done_r,
    right_a, left_b, right_q, right_i, left_o, right_o,
    load_sem, ends_send, ends_recv, z_send, z_recv, xy_send, xy_recv,
    back_send, back_recv, done_send, done_recv,
):
    seq = lax.axis_index("seq")
    ch = lax.axis_index("ch")
    y = seq // 32
    zh = (seq // 8) % 4
    s = seq % 8
    me = y * 8 + s
    z = zh * 2 + ch
    zbuf = (zbuf_f, zbuf_s)
    rows = (rows_f, rows_s)

    in_y = [(y + a) % 4 for a in range(4)]
    in_x = [(s // 2 + b) % 4 * 2 for b in range(4)]
    in_core = [s % 2, 1 - s % 2]

    def plane_peers():
        for a, b, e in PLANE:
            at = in_x[b] + in_core[e]
            yield in_y[a] * 8 + at, {"seq": in_y[a] * 32 + zh * 8 + at, "ch": ch}

    def z_device(to):
        return {"seq": y * 32 + (to // 2) * 8 + s, "ch": to % 2}

    def tile(i, n=8):
        return pl.ds(pl.multiple_of(i * n, n), n)

    def total(ref, sem):
        return pltpu.make_async_copy(ref, ref, sem)

    barrier = pltpu.get_barrier_semaphore()

    @pl.loop(0, 7)
    def _(i):
        pl.semaphore_signal(
            barrier, inc=1, device_id=z_device((z + 1 + (i + 3) % 7) % 8), device_id_type=MESH
        )

    for _, peer in plane_peers():
        pl.semaphore_signal(barrier, inc=1, device_id=peer, device_id_type=MESH)

    loads = [
        (filt, filt_v), (bias_h, bias), (key, key_v), (value, value_v), (taps_h, taps),
        (head_in_h, head_in), (turn4_h, turn4), (tail_in_h, tail_in),
        (block_in_h, block_in), (block_out_h.at[me % 2], block_out),
        (tail_out_h, tail_out), (turn2_h, turn2), (head_out2_h, head_out2), (head_out4_h, head_out4),
    ]
    loads = [pltpu.make_async_copy(a, b, load_sem.at[i]) for i, (a, b) in enumerate(loads)]
    for load in loads:
        load.start()
    drains = []
    pend = {}
    (l_filt, l_bias, l_key, l_value, l_taps, l_hi, l_turn, l_ti, l_bi, l_bo, l_to, l_t2, l_ho2, l_ho4) = loads

    l_filt.wait()
    l_bias.wait()
    for c in range(4):
        rows_f[c] = filt_v[pl.ds(c, 64, stride=4), :]
    first = jnp.where((lax.broadcasted_iota(jnp.int32, (1, 128), 1) == 0) & (seq == 0), 1.0, 0.0)
    for c in range(4):
        rows_f[c, 0:1, :] = rows_f[c, 0:1, :] + first * bias[c]

    l_key.wait()
    l_value.wait()
    l_taps.wait()
    for i, source in enumerate((key_v, value_v)):
        for c in range(4):
            ends_s[c, i : i + 1, :] = source[252 + c : 253 + c, :]
            ends_s[c, 2 + i : 3 + i, :] = source[c : c + 1, :]
    row = lax.broadcasted_iota(jnp.int32, (8, 128), 0) % 4
    lanes = lax.broadcasted_iota(jnp.int32, (256, 128), 1)

    def tap_rows(j, i):
        t = [taps[j, i, c] for c in range(4)]
        return jnp.where(row < 2, jnp.where(row == 0, t[0], t[1]), jnp.where(row == 2, t[2], t[3]))

    def short(source, i):
        x = source[...]
        result = None
        for j in range(3):
            t = tap_rows(j, i)
            moved = x
            if j > 0:
                near = pltpu.roll(x, j, 1)
                moved = jnp.where(lanes < j, pltpu.roll(near, 4, 0), near)
            term = t[None] * moved.reshape(32, 8, 128)
            result = term if result is None else result + term
        return result

    gate[...] = (short(key_v, 0) * short(value_v, 1)).reshape(256, 128)
    for c in range(4):
        rows_s[c] = gate[pl.ds(c, 64, stride=4), :]

    pl.semaphore_wait(barrier, 38)

    for i in (2, 3, 1):
        to = (zh + i) % 4
        pltpu.make_async_remote_copy(
            src_ref=ends_s.at[to],
            dst_ref=ends_z.at[zh],
            send_sem=ends_send.at[0],
            recv_sem=ends_recv.at[0],
            device_id=z_device(to * 2 + ch),
            device_id_type=MESH,
        ).start()
    drains.append(total(ends_s.at[0:3], ends_send.at[0]).wait)

    def z_exchange(f):
        for i in (2, 3, 1):
            to = (zh + i) % 4
            pltpu.make_async_remote_copy(
                src_ref=rows[f].at[to],
                dst_ref=zbuf[f].at[4 - i],
                send_sem=z_send.at[f],
                recv_sem=z_recv.at[f, 4 - i],
                device_id=z_device(to * 2 + ch),
                device_id_type=MESH,
            ).start()
            pend['z',f,4-i] = total(zbuf[f].at[4 - i], z_recv.at[f, 4 - i])
        drains.append(lambda: total(rows[f].at[0:3], z_send.at[f]).wait())

    z_exchange(0)
    z_exchange(1)
    ends_z[zh] = ends_s[zh]
    total(ends_z.at[0:3], ends_recv.at[0]).wait()

    @pl.loop(0, 4)
    def _(block):
        after = (y * 32 + block * 8 + s + 1) % 128
        pltpu.make_async_remote_copy(
            src_ref=ends_z.at[block],
            dst_ref=ends_r.at[(after // 8) % 4],
            send_sem=ends_send.at[1],
            recv_sem=ends_recv.at[1],
            device_id={"seq": (after // 32) * 32 + zh * 8 + after % 8, "ch": ch},
            device_id_type=MESH,
        ).start()

    pend['e'] = total(ends_r, ends_recv.at[1])
    drains.append(total(ends_z, ends_send.at[1]).wait)

    def first_rows():
        pend.pop('e').wait()
        lane = lax.broadcasted_iota(jnp.int32, (4, 128), 1)
        origin = lax.broadcasted_iota(jnp.int32, (4, 128), 0) + me == 0

        def whole(i):
            x = jnp.concatenate([ends_z[b, 2 + i : 3 + i, :] for b in range(4)], axis=0)
            before = jnp.concatenate([ends_r[b, i : i + 1, :] for b in range(4)], axis=0)
            before = jnp.where(origin, 0.0, before)
            result = taps[0, i, zh] * x
            for j in (1, 2):
                moved = jnp.where(lane < j, pltpu.roll(before, j, 1), pltpu.roll(x, j, 1))
                result = result + taps[j, i, zh] * moved
            return result

        fixed = whole(0) * whole(1)
        for b in range(4):
            starts[b, 0:1, :] = fixed[b : b + 1, :]

    for f in range(2):
        zbuf[f][0] = rows[f][zh]

    def forward(f, p):
        for d in FORWARD[p]:
            if d != 0:
                pend.pop(('z',f,d)).wait()
        if f == 1:
            if p == 0:
                first_rows()
            for d in FORWARD[p]:
                zbuf_s[d, 0:1, :] = starts[(zh + d) % 4, 0:1, :]
        put_split(right_a, jnp.concatenate([zbuf[f][d] for d in FORWARD[p]], axis=0), 0)
        if f == 0 and p == 0:
            l_hi.wait()
        real = mm(head_in[0:128, :], right_a[...])
        imag = mm(head_in[128:256, :], right_a[...])
        if f == 0 and p == 0:
            l_turn.wait()
            l_ti.wait()
        c, sn = turn4[:, 0:128], turn4[:, 128:256]
        turned = jnp.concatenate([real * c + imag * sn, imag * c - real * sn], axis=1)
        put_split(left_b, turned, 1)
        spread = mm(left_b[...], tail_in[...])
        for b in range(4):
            for i in range(2):
                sbuf[f, p, :, 2 * b + i, :] = spread[32 * b : 32 * b + 32, 128 * i : 128 * i + 128]
        for d, peer in plane_peers():
            pltpu.make_async_remote_copy(
                src_ref=sbuf.at[f, p, d],
                dst_ref=rbuf.at[f, p, me],
                send_sem=xy_send.at[f, p],
                recv_sem=xy_recv.at[f, p],
                device_id=peer,
                device_id_type=MESH,
            ).start()
        rbuf[f, p, me] = sbuf[f, p, me]
        pend['x',f,p] = total(rbuf.at[f, p, 0:31], xy_recv.at[f, p])
        drains.append(lambda: total(sbuf.at[f, p, 0:31], xy_send.at[f, p]).wait())

    def across(f):
        for p in range(2):
            pend.pop(('x',f,p)).wait()
            for n, d in enumerate(FORWARD[p]):
                for half in range(2):
                    at = n * 4 + half * 2
                    pair = [rbuf[f, p, :, at + i, :] for i in range(2)]
                    pair = jnp.concatenate(pair, axis=1)
                    high = pair.astype(BF16)
                    low = (pair - high.astype(F32)).astype(BF16)
                    base = (zh + d) % 4 * 64 + half * 32
                    for k, part in enumerate((high, low, high)):
                        right_q[pl.ds(pl.multiple_of(base + 256 * k, 32), 32), :] = part
        if f == 0:
            l_bi.wait()
        for m in range(0, 512, 128):
            cosines = mm(block_in[m : m + 128, :], right_q[...])
            sines = mm(block_in[512 + m : 640 + m, :], right_q[...])
            real = cosines[:, 0:128] + sines[:, 128:256]
            imag = cosines[:, 128:256] - sines[:, 0:128]
            if f == 0:
                spec[m : m + 128, 0:128] = real
                spec[m : m + 128, 128:256] = imag
            else:
                freal, fimag = spec[m : m + 128, 0:128], spec[m : m + 128, 128:256]
                prod = jnp.concatenate([real * freal - imag * fimag, real * fimag + imag * freal], axis=1)
                high = prod.astype(BF16)
                low = (prod - high.astype(F32)).astype(BF16)
                right_i[m : m + 128, :] = high
                right_i[512 + m : 640 + m, :] = low
                right_i[1024 + m : 1152 + m, :] = high

    forward(0, 0)
    forward(0, 1)
    forward(1, 0)
    forward(1, 1)
    across(0)
    across(1)
    l_bo.wait()

    def send_back(p):
        low, count = 64 * BACK[p][0], len(BACK[p])
        both = mm(block_out[low : low + 64 * count, :], right_i[...])
        for n in range(count):
            cosines, sines = both[64 * n : 64 * n + 32], both[64 * n + 32 : 64 * n + 64]
            back_s[p][:, 2 * n, :] = cosines[:, 0:128] - sines[:, 128:256]
            back_s[p][:, 2 * n + 1, :] = cosines[:, 128:256] + sines[:, 0:128]
        for d, peer in plane_peers():
            pltpu.make_async_remote_copy(
                src_ref=back_s[p].at[d],
                dst_ref=back_r[p].at[me],
                send_sem=back_send.at[p],
                recv_sem=back_recv.at[p],
                device_id=peer,
                device_id_type=MESH,
            ).start()
        back_r[p][me] = back_s[p][me]
        pend['b',p] = total(back_r[p].at[0:31], back_recv.at[p])
        drains.append(lambda: total(back_s[p].at[0:31], back_send.at[p]).wait())

    for p in range(len(BACK)):
        send_back(p)
    channel = ch * 4 + zh

    def finish_blocks(p):
        count = len(BACK[p])
        turn, head_out = (turn2, head_out2) if count == 2 else (turn4, head_out4)
        pend.pop(('b',p)).wait()
        high_low = []
        for i in range(2):
            for n in range(count):
                part = back_r[p][:, 2 * n + i, :]
                high = part.astype(BF16)
                low = (part - high.astype(F32)).astype(BF16)
                for k, piece in enumerate((high, low, high)):
                    left_o[32 * n : 32 * n + 32, 256 * k + 128 * i : 256 * k + 128 * i + 128] = piece
        if p == 0:
            l_to.wait()
            l_t2.wait()
            l_ho2.wait()
            l_ho4.wait()
        mixed = mm(left_o[0 : 32 * count, :], tail_out[...])
        c, sn = turn[:, 0:128], turn[:, 128:256]
        real, imag = mixed[:, 0:128], mixed[:, 128:256]
        right = right_o.at[0 : 192 * count]
        put_split(right, jnp.concatenate([real * c - imag * sn, real * sn + imag * c], axis=0), 0)
        low = 32 * BACK[p][0]
        done_s[low : low + 32 * count, :] = mm(head_out[...], right[...])
        for to in BACK[p]:
            block = done_s.at[32 * to : 32 * to + 32]

            @pl.when(to == z)
            def _():
                done_r[tile(channel, 32), :] = block[...]

            @pl.when(to != z)
            def _():
                pltpu.make_async_remote_copy(
                    src_ref=block,
                    dst_ref=done_r.at[tile(channel, 32)],
                    send_sem=done_send,
                    recv_sem=done_recv,
                    device_id=z_device(to),
                    device_id_type=MESH,
                ).start()

    for p in range(len(BACK)):
        finish_blocks(p)
    total(done_r.at[0:224], done_recv).wait()
    for j in range(32):
        out[8 * j : 8 * j + 8, :] = done_r[pl.ds(j, 8, stride=32), :]
    total(done_s.at[0:224], done_send).wait()
    for drain in drains:
        drain()


def by_time(x):
    return x.reshape(4, 64, 128).transpose(1, 0, 2).reshape(256, 128)


def local(query, key, value, filters, short_taps, bias):
    tables = make_tables()
    vm = pltpu.VMEM
    dma = pltpu.SemaphoreType.DMA
    table_scratch = [vm(t.shape if t.ndim == 2 else (512, 1536), t.dtype) for t in tables]
    conv = pl.pallas_call(
        kernel,
        out_shape=jax.ShapeDtypeStruct((256, 128), F32),
        in_specs=[pl.BlockSpec(memory_space=pl.ANY)] * 14,
        out_specs=pl.BlockSpec(memory_space=pltpu.VMEM),
        scratch_shapes=[vm((256, 128), F32)] * 3
        + [pltpu.SMEM((3, 2, 4), F32), pltpu.SMEM((4,), F32)]
        + table_scratch
        + [
            vm((256, 128), F32),
            vm((4, 8, 128), F32),
            vm((4, 8, 128), F32),
            vm((4, 8, 128), F32),
            vm((4, 8, 128), F32),
            vm((4, 64, 128), F32),
            vm((4, 64, 128), F32),
            vm((4, 64, 128), F32),
            vm((4, 64, 128), F32),
            vm((2, 2, 32, 8, 128), F32),
            vm((2, 2, 32, 8, 128), F32),
            vm((512, 256), F32),
            [vm((32, 2 * len(p), 128), F32) for p in BACK],
            [vm((32, 2 * len(p), 128), F32) for p in BACK],
            vm((256, 128), F32),
            vm((256, 128), F32),
            vm((384, 128), BF16),
            vm((128, 768), BF16),
            vm((768, 256), BF16),
            vm((1536, 256), BF16),
            vm((128, 768), BF16),
            vm((768, 128), BF16),
            dma((14,)),
            dma((2,)), dma((2,)),
            dma((2,)), dma((2, 4)),
            dma((2, 2)), dma((2, 2)),
            dma((3,)), dma((3,)),
            dma(()), dma(()),
        ],
        compiler_params=pltpu.CompilerParams(
            collective_id=0, has_side_effects=True, vmem_limit_bytes=56 * 1024 * 1024
        ),
        name="long_convolution",
    )(
        by_time(key), by_time(value), by_time(filters), short_taps.transpose(2, 0, 1), bias,
        *[jnp.asarray(t) for t in tables],
    )
    return conv.reshape(32, 8, 128).transpose(1, 0, 2).reshape(8, 4096) * query


def solution(mesh):
    return jax.shard_map(
        local,
        mesh=mesh,
        in_specs=(
            P(None, ("seq", "ch")),
            P("ch", "seq"),
            P("ch", "seq"),
            P("ch", "seq"),
            P(None, "ch", None),
            P("ch"),
        ),
        out_specs=P(None, ("seq", "ch")),
        check_vma=False,
    )
```

```python
import functools

import jax
import jax.numpy as jnp
import ml_dtypes
import numpy as np
from jax import lax
from jax.experimental import pallas as pl
from jax.experimental.pallas import tpu as pltpu
from jax.sharding import PartitionSpec as P

MESH = pl.DeviceIdType.MESH
F32 = jnp.float32
BF16 = jnp.bfloat16


def two_parts(table):
    high = table.astype(np.float32).astype(ml_dtypes.bfloat16)
    low = (table - high.astype(np.float64)).astype(np.float32).astype(ml_dtypes.bfloat16)
    return high, low


def as_left(table):
    high, low = two_parts(table)
    return np.concatenate([high, high, low], axis=1)


def as_right(table):
    high, low = two_parts(table)
    return np.concatenate([high, high, low], axis=0)


FORWARD = (
    (((0, 0), (0, 1)), ((1, 0), (1, 1), (3, 0), (3, 1)), ((2, 0), (2, 1))),
    (((0, 1), (2, 1)), ((0, 0), (2, 0)), ((1, 0), (1, 1), (3, 0), (3, 1))),
)
BACK = ((0, 1), (2, 3), (4, 5, 6, 7))
PLANE = sorted(
    ((a, b, e) for a in range(4) for b in range(4) for e in range(2) if (a, b, e) != (0, 0, 0)),
    key=lambda p: (-(2 - abs(2 - p[0])) - (2 - abs(2 - p[1])), p),
)


NEAR = [p for p in PLANE if p[:2] in ((0, 0), (0, 1), (0, 3), (1, 0), (3, 0))]


def make_tables():
    j1, k1 = np.arange(32), np.arange(32)
    lanes = np.arange(128)
    head = 2 * np.pi * np.outer(k1 + 0.5, j1) / 64
    step = np.stack([np.cos(head), -np.sin(head)])
    head_in = [np.einsum("rkj,ab->rakbj", step, np.eye(n)).reshape(64 * n, 32 * n) for n in (2, 4)]
    head_out = [np.einsum("rkj,ab->bjrak", step, np.eye(n)).reshape(32 * n, 64 * n) for n in (2, 4)]
    angle = 2 * np.pi * np.outer(k1 + 0.5, lanes) / 8192
    turn = np.concatenate([np.cos(angle), np.sin(angle)], axis=1).astype(np.float32)
    turn = [np.tile(turn, (n, 1)) for n in (2, 4)]
    tail = 2 * np.pi * np.outer(lanes, lanes) / 128
    c, s = np.cos(tail), np.sin(tail)
    tail_in = np.block([[c, -s], [s, c]])
    tail_out = np.block([[c, s], [-s, c]])
    place = np.arange(256).reshape(4, 4, 8, 2).transpose(1, 3, 0, 2).reshape(256)
    nu = np.arange(512)
    phase = 2 * np.pi * np.outer(nu, place) / 512
    block_in = np.concatenate([np.cos(phase), np.sin(phase)], axis=0)
    block_out = []
    for sign in (1, -1):
        wave = np.exp(1j * phase.T) * (1 + sign * 1j * np.exp(-2j * np.pi * nu / 512))[None, :]
        wave = wave.reshape(8, 32, 512) * 2.0**-21
        wave = np.stack([wave.real, wave.imag], axis=1).reshape(512, 512)
        block_out.append(as_left(wave))
    return (
        as_left(head_in[0]),
        as_left(head_in[1]),
        as_right(tail_in),
        turn[0],
        turn[1],
        as_left(block_in),
        np.stack(block_out),
        as_right(tail_out),
        as_left(head_out[0]),
        as_left(head_out[1]),
    )


def put_split(ref, value, axis):
    high = value.astype(BF16)
    low = (value - high.astype(F32)).astype(BF16)
    n = value.shape[axis]
    for place, part in enumerate((high, low, high)):
        if axis == 0:
            ref[place * n : (place + 1) * n, :] = part
        else:
            ref[:, place * n : (place + 1) * n] = part


def mm(a, b):
    return jnp.dot(a, b, preferred_element_type=F32)


def kernel(
    key, value, filt, taps_h, bias_h,
    head_in2_h, head_in4_h, tail_in_h, turn2_h, turn4_h, block_in_h, block_out_h, tail_out_h, head_out2_h, head_out4_h,
    out,
    key_v, value_v, filt_v, taps, bias,
    head_in2, head_in4, tail_in, turn2, turn4, block_in, block_out, tail_out, head_out2, head_out4,
    gate, ends_s, ends_z, ends_r, starts, rows_f, rows_s, zbuf_f, zbuf_s, sbuf, rbuf, spec, back_s, back_r, done_s, done_r,
    right_a, left_b, right_q, right_i, left_o, right_o,
    load_sem, ends_send, ends_recv, z_send, z_recv, xy_send, xy_recv,
    back_send, back_recv, done_send, done_recv, widen,
):
    seq = lax.axis_index("seq")
    ch = lax.axis_index("ch")
    y = seq // 32
    zh = (seq // 8) % 4
    s = seq % 8
    me = y * 8 + s
    z = zh * 2 + ch
    zbuf = (zbuf_f, zbuf_s)
    rows = (rows_f, rows_s)

    in_y = [(y + a) % 4 for a in range(4)]
    in_x = [(s // 2 + b) % 4 * 2 for b in range(4)]
    in_core = [s % 2, 1 - s % 2]

    def plane_peers(places=PLANE):
        for a, b, e in places:
            at = in_x[b] + in_core[e]
            yield in_y[a] * 8 + at, {"seq": in_y[a] * 32 + zh * 8 + at, "ch": ch}

    def z_device(to):
        return {"seq": y * 32 + (to // 2) * 8 + s, "ch": to % 2}

    def tile(i, n=8):
        return pl.ds(pl.multiple_of(i * n, n), n)

    def total(ref, sem):
        return pltpu.make_async_copy(ref, ref, sem)

    barrier = pltpu.get_barrier_semaphore()

    @pl.loop(0, 7)
    def _(i):
        pl.semaphore_signal(
            barrier, inc=1, device_id=z_device((z + 1 + (i + 3) % 7) % 8), device_id_type=MESH
        )

    for _, peer in plane_peers(NEAR):
        pl.semaphore_signal(barrier, inc=1, device_id=peer, device_id_type=MESH)

    loads = [
        (filt, filt_v), (bias_h, bias), (key, key_v), (value, value_v), (taps_h, taps),
        (head_in4_h, head_in4), (turn4_h, turn4), (tail_in_h, tail_in),
        (block_in_h, block_in), (block_out_h.at[me % 2], block_out),
        (tail_out_h, tail_out), (turn2_h, turn2), (head_in2_h, head_in2), (head_out2_h, head_out2), (head_out4_h, head_out4),
    ]
    loads = [pltpu.make_async_copy(a, b, load_sem.at[i]) for i, (a, b) in enumerate(loads)]
    for load in loads:
        load.start()
    drains = []
    pend = {}
    (l_filt, l_bias, l_key, l_value, l_taps, l_hi, l_turn, l_ti, l_bi, l_bo, l_to, l_t2, l_hi2, l_ho2, l_ho4) = loads

    l_filt.wait()
    l_bias.wait()
    for c in range(4):
        rows_f[c] = filt_v[pl.ds(c, 64, stride=4), :]
    first = jnp.where((lax.broadcasted_iota(jnp.int32, (1, 128), 1) == 0) & (seq == 0), 1.0, 0.0)
    for c in range(4):
        rows_f[c, 0:1, :] = rows_f[c, 0:1, :] + first * bias[c]

    l_key.wait()
    l_value.wait()
    l_taps.wait()
    for i, source in enumerate((key_v, value_v)):
        for c in range(4):
            ends_s[c, i : i + 1, :] = source[252 + c : 253 + c, :]
            ends_s[c, 2 + i : 3 + i, :] = source[c : c + 1, :]
    row = lax.broadcasted_iota(jnp.int32, (8, 128), 0) % 4
    lanes = lax.broadcasted_iota(jnp.int32, (256, 128), 1)

    def tap_rows(j, i):
        t = [taps[j, i, c] for c in range(4)]
        return jnp.where(row < 2, jnp.where(row == 0, t[0], t[1]), jnp.where(row == 2, t[2], t[3]))

    def short(source, i):
        x = source[...]
        result = None
        for j in range(3):
            t = tap_rows(j, i)
            moved = x
            if j > 0:
                near = pltpu.roll(x, j, 1)
                moved = jnp.where(lanes < j, pltpu.roll(near, 4, 0), near)
            term = t[None] * moved.reshape(32, 8, 128)
            result = term if result is None else result + term
        return result

    gate[...] = (short(key_v, 0) * short(value_v, 1)).reshape(256, 128)
    for c in range(4):
        rows_s[c] = gate[pl.ds(c, 64, stride=4), :]

    pl.semaphore_wait(barrier, 16)

    for i in (2, 3, 1):
        to = (zh + i) % 4
        pltpu.make_async_remote_copy(
            src_ref=ends_s.at[to],
            dst_ref=ends_z.at[zh],
            send_sem=ends_send.at[0],
            recv_sem=ends_recv.at[0],
            device_id=z_device(to * 2 + ch),
            device_id_type=MESH,
        ).start()
    drains.append(total(ends_s.at[0:3], ends_send.at[0]).wait)

    def z_exchange(f):
        for i in (2, 3, 1):
            to = (zh + i) % 4
            pltpu.make_async_remote_copy(
                src_ref=rows[f].at[to],
                dst_ref=zbuf[f].at[4 - i],
                send_sem=z_send.at[f],
                recv_sem=z_recv.at[f, 4 - i],
                device_id=z_device(to * 2 + ch),
                device_id_type=MESH,
            ).start()
            pend['z',f,4-i] = total(zbuf[f].at[4 - i], z_recv.at[f, 4 - i])
        drains.append(lambda: total(rows[f].at[0:3], z_send.at[f]).wait())

    z_exchange(0)
    z_exchange(1)
    for k in range(3):
        for _, peer in plane_peers(NEAR):
            pl.semaphore_signal(widen.at[k], inc=1, device_id=peer, device_id_type=MESH)
        pl.semaphore_wait(widen.at[k], 9)
    ends_z[zh] = ends_s[zh]
    total(ends_z.at[0:3], ends_recv.at[0]).wait()

    @pl.loop(0, 4)
    def _(block):
        after = (y * 32 + block * 8 + s + 1) % 128
        pltpu.make_async_remote_copy(
            src_ref=ends_z.at[block],
            dst_ref=ends_r.at[(after // 8) % 4],
            send_sem=ends_send.at[1],
            recv_sem=ends_recv.at[1],
            device_id={"seq": (after // 32) * 32 + zh * 8 + after % 8, "ch": ch},
            device_id_type=MESH,
        ).start()

    pend['e'] = total(ends_r, ends_recv.at[1])
    drains.append(total(ends_z, ends_send.at[1]).wait)

    def first_rows():
        pend.pop('e').wait()
        lane = lax.broadcasted_iota(jnp.int32, (4, 128), 1)
        origin = lax.broadcasted_iota(jnp.int32, (4, 128), 0) + me == 0

        def whole(i):
            x = jnp.concatenate([ends_z[b, 2 + i : 3 + i, :] for b in range(4)], axis=0)
            before = jnp.concatenate([ends_r[b, i : i + 1, :] for b in range(4)], axis=0)
            before = jnp.where(origin, 0.0, before)
            result = taps[0, i, zh] * x
            for j in (1, 2):
                moved = jnp.where(lane < j, pltpu.roll(before, j, 1), pltpu.roll(x, j, 1))
                result = result + taps[j, i, zh] * moved
            return result

        fixed = whole(0) * whole(1)
        for b in range(4):
            starts[b, 0:1, :] = fixed[b : b + 1, :]

    for f in range(2):
        zbuf[f][0] = rows[f][zh]

    def forward(f, p):
        which = FORWARD[f][p]
        count = len(which)
        head_in, turn = (head_in2, turn2) if count == 2 else (head_in4, turn4)
        for d, half in which:
            if ('z', f, d) in pend:
                pend.pop(('z',f,d)).wait()
            if f == 1 and half == 0:
                if 'e' in pend:
                    first_rows()
                zbuf_s[d, 0:1, :] = starts[(zh + d) % 4, 0:1, :]
        blocks = [zbuf[f][d, 32 * half : 32 * half + 32, :] for d, half in which]
        right = right_a.at[0 : 96 * count]
        put_split(right, jnp.concatenate(blocks, axis=0), 0)
        if f == 0 and p == 1:
            l_hi.wait()
            l_turn.wait()
        real = mm(head_in[0 : 32 * count, :], right[...])
        imag = mm(head_in[32 * count : 64 * count, :], right[...])
        if f == 0 and p == 0:
            l_ti.wait()
        c, sn = turn[:, 0:128], turn[:, 128:256]
        turned = jnp.concatenate([real * c + imag * sn, imag * c - real * sn], axis=1)
        left = left_b.at[0 : 32 * count]
        put_split(left, turned, 1)
        spread = mm(left[...], tail_in[...])
        for b in range(count):
            for i in range(2):
                sbuf[f][p][:, 2 * b + i, :] = spread[32 * b : 32 * b + 32, 128 * i : 128 * i + 128]
        for d, peer in plane_peers():
            pltpu.make_async_remote_copy(
                src_ref=sbuf[f][p].at[d],
                dst_ref=rbuf[f][p].at[me],
                send_sem=xy_send.at[f, p],
                recv_sem=xy_recv.at[f, p],
                device_id=peer,
                device_id_type=MESH,
            ).start()
        rbuf[f][p][me] = sbuf[f][p][me]
        pend['x',f,p] = total(rbuf[f][p].at[0:31], xy_recv.at[f, p])
        drains.append(lambda: total(sbuf[f][p].at[0:31], xy_send.at[f, p]).wait())

    def across(f):
        for p in range(len(FORWARD[f])):
            pend.pop(('x',f,p)).wait()
            for n, (d, half) in enumerate(FORWARD[f][p]):
                pair = [rbuf[f][p][:, 2 * n + i, :] for i in range(2)]
                pair = jnp.concatenate(pair, axis=1)
                high = pair.astype(BF16)
                low = (pair - high.astype(F32)).astype(BF16)
                base = (zh + d) % 4 * 64 + half * 32
                for k, part in enumerate((high, low, high)):
                    right_q[pl.ds(pl.multiple_of(base + 256 * k, 32), 32), :] = part
        if f == 0:
            l_bi.wait()
        for m in range(0, 512, 128):
            cosines = mm(block_in[m : m + 128, :], right_q[...])
            sines = mm(block_in[512 + m : 640 + m, :], right_q[...])
            real = cosines[:, 0:128] + sines[:, 128:256]
            imag = cosines[:, 128:256] - sines[:, 0:128]
            if f == 0:
                spec[m : m + 128, 0:128] = real
                spec[m : m + 128, 128:256] = imag
            else:
                freal, fimag = spec[m : m + 128, 0:128], spec[m : m + 128, 128:256]
                prod = jnp.concatenate([real * freal - imag * fimag, real * fimag + imag * freal], axis=1)
                high = prod.astype(BF16)
                low = (prod - high.astype(F32)).astype(BF16)
                right_i[m : m + 128, :] = high
                right_i[512 + m : 640 + m, :] = low
                right_i[1024 + m : 1152 + m, :] = high

    l_t2.wait()
    l_hi2.wait()
    for f in range(2):
        for p in range(len(FORWARD[f])):
            forward(f, p)
    across(0)
    across(1)
    l_bo.wait()

    def send_back(p):
        low, count = 64 * BACK[p][0], len(BACK[p])
        both = mm(block_out[low : low + 64 * count, :], right_i[...])
        for n in range(count):
            cosines, sines = both[64 * n : 64 * n + 32], both[64 * n + 32 : 64 * n + 64]
            back_s[p][:, 2 * n, :] = cosines[:, 0:128] - sines[:, 128:256]
            back_s[p][:, 2 * n + 1, :] = cosines[:, 128:256] + sines[:, 0:128]
        for d, peer in plane_peers():
            pltpu.make_async_remote_copy(
                src_ref=back_s[p].at[d],
                dst_ref=back_r[p].at[me],
                send_sem=back_send.at[p],
                recv_sem=back_recv.at[p],
                device_id=peer,
                device_id_type=MESH,
            ).start()
        back_r[p][me] = back_s[p][me]
        pend['b',p] = total(back_r[p].at[0:31], back_recv.at[p])
        drains.append(lambda: total(back_s[p].at[0:31], back_send.at[p]).wait())

    for p in range(len(BACK)):
        send_back(p)
    channel = ch * 4 + zh

    def finish_blocks(p):
        count = len(BACK[p])
        turn, head_out = (turn2, head_out2) if count == 2 else (turn4, head_out4)
        pend.pop(('b',p)).wait()
        high_low = []
        for i in range(2):
            for n in range(count):
                part = back_r[p][:, 2 * n + i, :]
                high = part.astype(BF16)
                low = (part - high.astype(F32)).astype(BF16)
                for k, piece in enumerate((high, low, high)):
                    left_o[32 * n : 32 * n + 32, 256 * k + 128 * i : 256 * k + 128 * i + 128] = piece
        if p == 0:
            l_to.wait()
            l_ho2.wait()
            l_ho4.wait()
        mixed = mm(left_o[0 : 32 * count, :], tail_out[...])
        c, sn = turn[:, 0:128], turn[:, 128:256]
        real, imag = mixed[:, 0:128], mixed[:, 128:256]
        right = right_o.at[0 : 192 * count]
        put_split(right, jnp.concatenate([real * c - imag * sn, real * sn + imag * c], axis=0), 0)
        low = 32 * BACK[p][0]
        done_s[low : low + 32 * count, :] = mm(head_out[...], right[...])
        for to in BACK[p]:
            block = done_s.at[32 * to : 32 * to + 32]

            @pl.when(to == z)
            def _():
                done_r[tile(channel, 32), :] = block[...]

            @pl.when(to != z)
            def _():
                pltpu.make_async_remote_copy(
                    src_ref=block,
                    dst_ref=done_r.at[tile(channel, 32)],
                    send_sem=done_send,
                    recv_sem=done_recv,
                    device_id=z_device(to),
                    device_id_type=MESH,
                ).start()

    for p in range(len(BACK)):
        finish_blocks(p)
    total(done_r.at[0:224], done_recv).wait()
    for j in range(32):
        out[8 * j : 8 * j + 8, :] = done_r[pl.ds(j, 8, stride=32), :]
    total(done_s.at[0:224], done_send).wait()
    for drain in drains:
        drain()


def by_time(x):
    return x.reshape(4, 64, 128).transpose(1, 0, 2).reshape(256, 128)


def local(query, key, value, filters, short_taps, bias):
    tables = make_tables()
    vm = pltpu.VMEM
    dma = pltpu.SemaphoreType.DMA
    table_scratch = [vm(t.shape if t.ndim == 2 else (512, 1536), t.dtype) for t in tables]
    conv = pl.pallas_call(
        kernel,
        out_shape=jax.ShapeDtypeStruct((256, 128), F32),
        in_specs=[pl.BlockSpec(memory_space=pl.ANY)] * 15,
        out_specs=pl.BlockSpec(memory_space=pltpu.VMEM),
        scratch_shapes=[vm((256, 128), F32)] * 3
        + [pltpu.SMEM((3, 2, 4), F32), pltpu.SMEM((4,), F32)]
        + table_scratch
        + [
            vm((256, 128), F32),
            vm((4, 8, 128), F32),
            vm((4, 8, 128), F32),
            vm((4, 8, 128), F32),
            vm((4, 8, 128), F32),
            vm((4, 64, 128), F32),
            vm((4, 64, 128), F32),
            vm((4, 64, 128), F32),
            vm((4, 64, 128), F32),
            [[vm((32, 2 * len(p), 128), F32) for p in pieces] for pieces in FORWARD],
            [[vm((32, 2 * len(p), 128), F32) for p in pieces] for pieces in FORWARD],
            vm((512, 256), F32),
            [vm((32, 2 * len(p), 128), F32) for p in BACK],
            [vm((32, 2 * len(p), 128), F32) for p in BACK],
            vm((256, 128), F32),
            vm((256, 128), F32),
            vm((384, 128), BF16),
            vm((128, 768), BF16),
            vm((768, 256), BF16),
            vm((1536, 256), BF16),
            vm((128, 768), BF16),
            vm((768, 128), BF16),
            dma((15,)),
            dma((2,)), dma((2,)),
            dma((2,)), dma((2, 4)),
            dma((2, 3)), dma((2, 3)),
            dma((3,)), dma((3,)),
            dma(()), dma(()),
            pltpu.SemaphoreType.REGULAR((3,)),
        ],
        compiler_params=pltpu.CompilerParams(
            collective_id=0, has_side_effects=True, vmem_limit_bytes=56 * 1024 * 1024
        ),
        name="long_convolution",
    )(
        by_time(key), by_time(value), by_time(filters), short_taps.transpose(2, 0, 1), bias,
        *[jnp.asarray(t) for t in tables],
    )
    return conv.reshape(32, 8, 128).transpose(1, 0, 2).reshape(8, 4096) * query


def solution(mesh):
    return jax.shard_map(
        local,
        mesh=mesh,
        in_specs=(
            P(None, ("seq", "ch")),
            P("ch", "seq"),
            P("ch", "seq"),
            P("ch", "seq"),
            P(None, "ch", None),
            P("ch"),
        ),
        out_specs=P(None, ("seq", "ch")),
        check_vma=False,
    )
```

```python
import functools

import jax
import jax.numpy as jnp
import ml_dtypes
import numpy as np
from jax import lax
from jax.experimental import pallas as pl
from jax.experimental.pallas import tpu as pltpu
from jax.sharding import PartitionSpec as P

MESH = pl.DeviceIdType.MESH
F32 = jnp.float32
BF16 = jnp.bfloat16


def two_parts(table):
    high = table.astype(np.float32).astype(ml_dtypes.bfloat16)
    low = (table - high.astype(np.float64)).astype(np.float32).astype(ml_dtypes.bfloat16)
    return high, low


def as_left(table):
    high, low = two_parts(table)
    return np.concatenate([high, high, low], axis=1)


def as_right(table):
    high, low = two_parts(table)
    return np.concatenate([high, high, low], axis=0)


FORWARD = (
    (((0, 0), (0, 1)), ((1, 0), (1, 1), (3, 0), (3, 1)), ((2, 0), (2, 1))),
    (((0, 1), (2, 1)), ((0, 0), (2, 0)), ((1, 0), (1, 1), (3, 0), (3, 1))),
)
BACK = ((0, 1), (2, 3), (4, 5, 6, 7))
PLANE = sorted(
    ((a, b, e) for a in range(4) for b in range(4) for e in range(2) if (a, b, e) != (0, 0, 0)),
    key=lambda p: (-(2 - abs(2 - p[0])) - (2 - abs(2 - p[1])), p),
)


NEAR = [p for p in PLANE if p[:2] in ((0, 0), (0, 1), (0, 3), (1, 0), (3, 0))]


def make_tables():
    j1, k1 = np.arange(32), np.arange(32)
    lanes = np.arange(128)
    head = 2 * np.pi * np.outer(k1 + 0.5, j1) / 64
    step = np.stack([np.cos(head), -np.sin(head)])
    head_in = [np.einsum("rkj,ab->rakbj", step, np.eye(n)).reshape(64 * n, 32 * n) for n in (2, 4)]
    head_out = [np.einsum("rkj,ab->bjrak", step, np.eye(n)).reshape(32 * n, 64 * n) for n in (2, 4)]
    angle = 2 * np.pi * np.outer(k1 + 0.5, lanes) / 8192
    turn = np.concatenate([np.cos(angle), np.sin(angle)], axis=1).astype(np.float32)
    turn = [np.tile(turn, (n, 1)) for n in (2, 4)]
    tail = 2 * np.pi * np.outer(lanes, lanes) / 128
    c, s = np.cos(tail), np.sin(tail)
    tail_in = np.block([[c, -s], [s, c]])
    tail_out = np.block([[c, s], [-s, c]])
    place = np.arange(256).reshape(4, 4, 8, 2).transpose(1, 3, 0, 2).reshape(256)
    nu = np.arange(256)
    phase = 2 * np.pi * np.outer(nu, place) / 512
    cosines, sines = np.cos(phase), np.sin(phase)
    sines[0] = np.cos(np.pi * place)
    block_in = np.concatenate([cosines, sines], axis=0)
    block_out = block_in.T * 2.0**-21
    shift = np.stack([np.sin(2 * np.pi * nu / 512), np.cos(2 * np.pi * nu / 512), np.cos(2 * np.pi * nu / 512)])
    shift[2, 0] = -1.0
    shift = np.repeat(shift, 128, axis=0).T.astype(np.float32)
    return (
        as_left(head_in[0]),
        as_left(head_in[1]),
        as_right(tail_in),
        turn[0],
        turn[1],
        as_left(block_in),
        as_left(block_out),
        shift,
        as_right(tail_out),
        as_left(head_out[0]),
        as_left(head_out[1]),
    )


def put_split(ref, value, axis):
    high = value.astype(BF16)
    low = (value - high.astype(F32)).astype(BF16)
    n = value.shape[axis]
    for place, part in enumerate((high, low, high)):
        if axis == 0:
            ref[place * n : (place + 1) * n, :] = part
        else:
            ref[:, place * n : (place + 1) * n] = part


def mm(a, b):
    return jnp.dot(a, b, preferred_element_type=F32)


def kernel(
    key, value, filt, taps_h, bias_h,
    head_in2_h, head_in4_h, tail_in_h, turn2_h, turn4_h, block_in_h, block_out_h, shift_h, tail_out_h, head_out2_h, head_out4_h,
    out,
    key_v, value_v, filt_v, taps, bias,
    head_in2, head_in4, tail_in, turn2, turn4, block_in, block_out, shift, tail_out, head_out2, head_out4,
    gate, ends_s, ends_z, ends_r, starts, rows_f, rows_s, zbuf_f, zbuf_s, sbuf, rbuf, spec, back_s, back_r, done_s,
    right_a, left_b, right_q, right_i, left_o, right_o,
    load_sem, ends_send, ends_recv, z_send, z_recv, xy_send, xy_recv,
    back_send, back_recv, done_send, done_recv, widen,
):
    seq = lax.axis_index("seq")
    ch = lax.axis_index("ch")
    y = seq // 32
    zh = (seq // 8) % 4
    s = seq % 8
    me = y * 8 + s
    z = zh * 2 + ch
    zbuf = (zbuf_f, zbuf_s)
    rows = (rows_f, rows_s)

    in_y = [(y + a) % 4 for a in range(4)]
    in_x = [(s // 2 + b) % 4 * 2 for b in range(4)]
    in_core = [s % 2, 1 - s % 2]

    def plane_peers(places=PLANE):
        for a, b, e in places:
            at = in_x[b] + in_core[e]
            yield in_y[a] * 8 + at, {"seq": in_y[a] * 32 + zh * 8 + at, "ch": ch}

    def z_device(to):
        return {"seq": y * 32 + (to // 2) * 8 + s, "ch": to % 2}

    def tile(i, n=8):
        return pl.ds(pl.multiple_of(i * n, n), n)

    def total(ref, sem):
        return pltpu.make_async_copy(ref, ref, sem)

    barrier = pltpu.get_barrier_semaphore()

    @pl.loop(0, 7)
    def _(i):
        pl.semaphore_signal(
            barrier, inc=1, device_id=z_device((z + 1 + (i + 3) % 7) % 8), device_id_type=MESH
        )

    for _, peer in plane_peers(NEAR):
        pl.semaphore_signal(barrier, inc=1, device_id=peer, device_id_type=MESH)

    loads = [
        (filt, filt_v), (bias_h, bias), (key, key_v), (value, value_v), (taps_h, taps),
        (head_in4_h, head_in4), (turn4_h, turn4), (tail_in_h, tail_in),
        (block_in_h, block_in), (shift_h, shift), (block_out_h, block_out),
        (tail_out_h, tail_out), (turn2_h, turn2), (head_in2_h, head_in2), (head_out2_h, head_out2), (head_out4_h, head_out4),
    ]
    loads = [pltpu.make_async_copy(a, b, load_sem.at[i]) for i, (a, b) in enumerate(loads)]
    for load in loads:
        load.start()
    drains = []
    pend = {}
    (l_filt, l_bias, l_key, l_value, l_taps, l_hi, l_turn, l_ti, l_bi, l_sh, l_bo, l_to, l_t2, l_hi2, l_ho2, l_ho4) = loads

    l_filt.wait()
    l_bias.wait()
    for c in range(4):
        rows_f[c] = filt_v[pl.ds(c, 64, stride=4), :]
    first = jnp.where((lax.broadcasted_iota(jnp.int32, (1, 128), 1) == 0) & (seq == 0), 1.0, 0.0)
    for c in range(4):
        rows_f[c, 0:1, :] = rows_f[c, 0:1, :] + first * bias[c]

    l_key.wait()
    l_value.wait()
    l_taps.wait()
    for i, source in enumerate((key_v, value_v)):
        for c in range(4):
            ends_s[c, i : i + 1, :] = source[252 + c : 253 + c, :]
            ends_s[c, 2 + i : 3 + i, :] = source[c : c + 1, :]
    row = lax.broadcasted_iota(jnp.int32, (8, 128), 0) % 4
    lanes = lax.broadcasted_iota(jnp.int32, (256, 128), 1)

    def tap_rows(j, i):
        t = [taps[j, i, c] for c in range(4)]
        return jnp.where(row < 2, jnp.where(row == 0, t[0], t[1]), jnp.where(row == 2, t[2], t[3]))

    def short(source, i):
        x = source[...]
        result = None
        for j in range(3):
            t = tap_rows(j, i)
            moved = x
            if j > 0:
                near = pltpu.roll(x, j, 1)
                moved = jnp.where(lanes < j, pltpu.roll(near, 4, 0), near)
            term = t[None] * moved.reshape(32, 8, 128)
            result = term if result is None else result + term
        return result

    gate[...] = (short(key_v, 0) * short(value_v, 1)).reshape(256, 128)
    for c in range(4):
        rows_s[c] = gate[pl.ds(c, 64, stride=4), :]

    pl.semaphore_wait(barrier, 16)

    for i in (2, 3, 1):
        to = (zh + i) % 4
        pltpu.make_async_remote_copy(
            src_ref=ends_s.at[to],
            dst_ref=ends_z.at[zh],
            send_sem=ends_send.at[0],
            recv_sem=ends_recv.at[0],
            device_id=z_device(to * 2 + ch),
            device_id_type=MESH,
        ).start()
    drains.append(total(ends_s.at[0:3], ends_send.at[0]).wait)

    def z_exchange(f):
        for i in (2, 3, 1):
            to = (zh + i) % 4
            pltpu.make_async_remote_copy(
                src_ref=rows[f].at[to],
                dst_ref=zbuf[f].at[4 - i],
                send_sem=z_send.at[f],
                recv_sem=z_recv.at[f, 4 - i],
                device_id=z_device(to * 2 + ch),
                device_id_type=MESH,
            ).start()
            pend['z',f,4-i] = total(zbuf[f].at[4 - i], z_recv.at[f, 4 - i])
        drains.append(lambda: total(rows[f].at[0:3], z_send.at[f]).wait())

    z_exchange(0)
    z_exchange(1)
    for k in range(3):
        for _, peer in plane_peers(NEAR):
            pl.semaphore_signal(widen.at[k], inc=1, device_id=peer, device_id_type=MESH)
        pl.semaphore_wait(widen.at[k], 9)
    ends_z[zh] = ends_s[zh]
    total(ends_z.at[0:3], ends_recv.at[0]).wait()

    @pl.loop(0, 4)
    def _(block):
        after = (y * 32 + block * 8 + s + 1) % 128
        pltpu.make_async_remote_copy(
            src_ref=ends_z.at[block],
            dst_ref=ends_r.at[(after // 8) % 4],
            send_sem=ends_send.at[1],
            recv_sem=ends_recv.at[1],
            device_id={"seq": (after // 32) * 32 + zh * 8 + after % 8, "ch": ch},
            device_id_type=MESH,
        ).start()

    pend['e'] = total(ends_r, ends_recv.at[1])
    drains.append(total(ends_z, ends_send.at[1]).wait)

    def first_rows():
        pend.pop('e').wait()
        lane = lax.broadcasted_iota(jnp.int32, (4, 128), 1)
        origin = lax.broadcasted_iota(jnp.int32, (4, 128), 0) + me == 0

        def whole(i):
            x = jnp.concatenate([ends_z[b, 2 + i : 3 + i, :] for b in range(4)], axis=0)
            before = jnp.concatenate([ends_r[b, i : i + 1, :] for b in range(4)], axis=0)
            before = jnp.where(origin, 0.0, before)
            result = taps[0, i, zh] * x
            for j in (1, 2):
                moved = jnp.where(lane < j, pltpu.roll(before, j, 1), pltpu.roll(x, j, 1))
                result = result + taps[j, i, zh] * moved
            return result

        fixed = whole(0) * whole(1)
        for b in range(4):
            starts[b, 0:1, :] = fixed[b : b + 1, :]

    for f in range(2):
        zbuf[f][0] = rows[f][zh]

    def forward(f, p):
        which = FORWARD[f][p]
        count = len(which)
        head_in, turn = (head_in2, turn2) if count == 2 else (head_in4, turn4)
        for d, half in which:
            if ('z', f, d) in pend:
                pend.pop(('z',f,d)).wait()
            if f == 1 and half == 0:
                if 'e' in pend:
                    first_rows()
                zbuf_s[d, 0:1, :] = starts[(zh + d) % 4, 0:1, :]
        blocks = [zbuf[f][d, 32 * half : 32 * half + 32, :] for d, half in which]
        right = right_a.at[0 : 96 * count]
        put_split(right, jnp.concatenate(blocks, axis=0), 0)
        if f == 0 and p == 1:
            l_hi.wait()
            l_turn.wait()
        real = mm(head_in[0 : 32 * count, :], right[...])
        imag = mm(head_in[32 * count : 64 * count, :], right[...])
        if f == 0 and p == 0:
            l_ti.wait()
        c, sn = turn[:, 0:128], turn[:, 128:256]
        turned = jnp.concatenate([real * c + imag * sn, imag * c - real * sn], axis=1)
        left = left_b.at[0 : 32 * count]
        put_split(left, turned, 1)
        spread = mm(left[...], tail_in[...])
        for b in range(count):
            for i in range(2):
                sbuf[f][p][:, 2 * b + i, :] = spread[32 * b : 32 * b + 32, 128 * i : 128 * i + 128]
        for d, peer in plane_peers():
            pltpu.make_async_remote_copy(
                src_ref=sbuf[f][p].at[d],
                dst_ref=rbuf[f][p].at[me],
                send_sem=xy_send.at[f, p],
                recv_sem=xy_recv.at[f, p],
                device_id=peer,
                device_id_type=MESH,
            ).start()
        rbuf[f][p][me] = sbuf[f][p][me]
        pend['x',f,p] = total(rbuf[f][p].at[0:31], xy_recv.at[f, p])
        drains.append(lambda: total(sbuf[f][p].at[0:31], xy_send.at[f, p]).wait())

    top_row = lax.broadcasted_iota(jnp.int32, (128, 128), 0) == 0
    sign = jnp.where(me % 2 == 0, 1.0, -1.0)

    def times(a, b):
        return a[0] * b[0] - a[1] * b[1], a[0] * b[1] + a[1] * b[0]

    def across(f):
        for p in range(len(FORWARD[f])):
            pend.pop(('x',f,p)).wait()
            for n, (d, half) in enumerate(FORWARD[f][p]):
                pair = [rbuf[f][p][:, 2 * n + i, :] for i in range(2)]
                pair = jnp.concatenate(pair, axis=1)
                high = pair.astype(BF16)
                low = (pair - high.astype(F32)).astype(BF16)
                base = (zh + d) % 4 * 64 + half * 32
                for k, part in enumerate((high, low, high)):
                    right_q[pl.ds(pl.multiple_of(base + 256 * k, 32), 32), :] = part
        if f == 0:
            l_bi.wait()
            l_sh.wait()
        for m in range(0, 256, 128):
            part = slice(m, m + 128)
            cosines = mm(block_in[part, :], right_q[...])
            sines = mm(block_in[256 + m : 384 + m, :], right_q[...])
            cre, cim, sre, sim = cosines[:, 0:128], cosines[:, 128:256], sines[:, 0:128], sines[:, 128:256]

            def alone(first, other):
                return jnp.where(top_row, first, other) if m == 0 else other

            up = alone(cre, cre + sim), alone(cim, cim - sre)
            down = alone(sre, cre - sim), alone(sim, cim + sre)
            if f == 0:
                tilt = sign * shift[part, 0:128]
                up = times(up, (1.0 + tilt, sign * shift[part, 128:256]))
                down = times(down, (1.0 - tilt, sign * shift[part, 256:384]))
                for k, x in enumerate(up + down):
                    spec[part, 128 * k : 128 * k + 128] = x
            else:
                up = times(up, (spec[part, 0:128], spec[part, 128:256]))
                down = times(down, (spec[part, 256:384], spec[part, 384:512]))
                even = [alone(up[k], up[k] + down[k]) for k in range(2)]
                odd = [alone(down[0], down[1] - up[1]), alone(down[1], up[0] - down[0])]
                for at, pair in ((m, even), (256 + m, odd)):
                    pair = jnp.concatenate(pair, axis=1)
                    high = pair.astype(BF16)
                    low = (pair - high.astype(F32)).astype(BF16)
                    for k, x in enumerate((high, low, high)):
                        right_i[512 * k + at : 512 * k + at + 128, :] = x

    l_t2.wait()
    l_hi2.wait()
    for f in range(2):
        for p in range(len(FORWARD[f])):
            forward(f, p)
    across(0)
    across(1)
    l_bo.wait()

    def send_back(p):
        low, count = 32 * BACK[p][0], len(BACK[p])
        both = mm(block_out[low : low + 32 * count, :], right_i[...])
        for n in range(count):
            for i in range(2):
                back_s[p][:, 2 * n + i, :] = both[32 * n : 32 * n + 32, 128 * i : 128 * i + 128]
        for d, peer in plane_peers():
            pltpu.make_async_remote_copy(
                src_ref=back_s[p].at[d],
                dst_ref=back_r[p].at[me],
                send_sem=back_send.at[p],
                recv_sem=back_recv.at[p],
                device_id=peer,
                device_id_type=MESH,
            ).start()
        back_r[p][me] = back_s[p][me]
        pend['b',p] = total(back_r[p].at[0:31], back_recv.at[p])
        drains.append(lambda: total(back_s[p].at[0:31], back_send.at[p]).wait())

    for p in range(len(BACK)):
        send_back(p)
    channel = ch * 4 + zh

    def finish_blocks(p):
        count = len(BACK[p])
        turn, head_out = (turn2, head_out2) if count == 2 else (turn4, head_out4)
        pend.pop(('b',p)).wait()
        high_low = []
        for i in range(2):
            for n in range(count):
                part = back_r[p][:, 2 * n + i, :]
                high = part.astype(BF16)
                low = (part - high.astype(F32)).astype(BF16)
                for k, piece in enumerate((high, low, high)):
                    left_o[32 * n : 32 * n + 32, 256 * k + 128 * i : 256 * k + 128 * i + 128] = piece
        if p == 0:
            l_to.wait()
            l_ho2.wait()
            l_ho4.wait()
        mixed = mm(left_o[0 : 32 * count, :], tail_out[...])
        c, sn = turn[:, 0:128], turn[:, 128:256]
        real, imag = mixed[:, 0:128], mixed[:, 128:256]
        right = right_o.at[0 : 192 * count]
        put_split(right, jnp.concatenate([real * c - imag * sn, real * sn + imag * c], axis=0), 0)
        low = 32 * BACK[p][0]
        done_s[low : low + 32 * count, :] = mm(head_out[...], right[...])
        for to in BACK[p]:
            block = done_s.at[32 * to : 32 * to + 32]

            @pl.when(to == z)
            def _():
                pltpu.make_async_copy(block, out.at[tile(channel, 32)], done_recv).start()

            @pl.when(to != z)
            def _():
                pltpu.make_async_remote_copy(
                    src_ref=block,
                    dst_ref=out.at[tile(channel, 32)],
                    send_sem=done_send,
                    recv_sem=done_recv,
                    device_id=z_device(to),
                    device_id_type=MESH,
                ).start()

    for p in range(len(BACK)):
        finish_blocks(p)
    total(out, done_recv).wait()
    total(done_s.at[0:224], done_send).wait()
    for drain in drains:
        drain()


def mix(conv, query, out, conv_v, query_v, out_v, sem):
    loads, stores = [], []
    for k in range(4):
        lanes = pl.ds(1024 * k, 1024)
        loads.append((
            pltpu.make_async_copy(conv.at[:, 8 * k : 8 * k + 8], conv_v.at[k], sem.at[0, k]),
            pltpu.make_async_copy(query.at[:, lanes], query_v.at[:, lanes], sem.at[1, k]),
        ))
        stores.append(pltpu.make_async_copy(out_v.at[:, lanes], out.at[:, lanes], sem.at[2, k]))
        for load in loads[k]:
            load.start()
    for k in range(4):
        for load in loads[k]:
            load.wait()
        for j in range(8):
            lanes = slice(1024 * k + 128 * j, 1024 * k + 128 * j + 128)
            out_v[:, lanes] = conv_v[k, :, j, :] * query_v[:, lanes]
        stores[k].start()
    for store in stores:
        store.wait()


def by_time(x):
    return x.reshape(4, 64, 128).transpose(1, 0, 2).reshape(256, 128)


def local(query, key, value, filters, short_taps, bias):
    tables = make_tables()
    vm = pltpu.VMEM
    dma = pltpu.SemaphoreType.DMA
    table_scratch = [vm(t.shape, t.dtype) for t in tables]
    conv = pl.pallas_call(
        kernel,
        out_shape=jax.ShapeDtypeStruct((256, 128), F32),
        in_specs=[pl.BlockSpec(memory_space=pl.ANY)] * 16,
        out_specs=pl.BlockSpec(memory_space=pl.ANY),
        scratch_shapes=[vm((256, 128), F32)] * 3
        + [pltpu.SMEM((3, 2, 4), F32), pltpu.SMEM((4,), F32)]
        + table_scratch
        + [
            vm((256, 128), F32),
            vm((4, 8, 128), F32),
            vm((4, 8, 128), F32),
            vm((4, 8, 128), F32),
            vm((4, 8, 128), F32),
            vm((4, 64, 128), F32),
            vm((4, 64, 128), F32),
            vm((4, 64, 128), F32),
            vm((4, 64, 128), F32),
            [[vm((32, 2 * len(p), 128), F32) for p in pieces] for pieces in FORWARD],
            [[vm((32, 2 * len(p), 128), F32) for p in pieces] for pieces in FORWARD],
            vm((256, 512), F32),
            [vm((32, 2 * len(p), 128), F32) for p in BACK],
            [vm((32, 2 * len(p), 128), F32) for p in BACK],
            vm((256, 128), F32),
            vm((384, 128), BF16),
            vm((128, 768), BF16),
            vm((768, 256), BF16),
            vm((1536, 256), BF16),
            vm((128, 768), BF16),
            vm((768, 128), BF16),
            dma((16,)),
            dma((2,)), dma((2,)),
            dma((2,)), dma((2, 4)),
            dma((2, 3)), dma((2, 3)),
            dma((3,)), dma((3,)),
            dma(()), dma(()),
            pltpu.SemaphoreType.REGULAR((3,)),
        ],
        compiler_params=pltpu.CompilerParams(
            collective_id=0, has_side_effects=True, vmem_limit_bytes=56 * 1024 * 1024
        ),
        name="long_convolution",
    )(
        by_time(key), by_time(value), by_time(filters), short_taps.transpose(2, 0, 1), bias,
        *[jnp.asarray(t) for t in tables],
    )
    return pl.pallas_call(
        mix,
        out_shape=jax.ShapeDtypeStruct((8, 4096), F32),
        in_specs=[pl.BlockSpec(memory_space=pl.ANY)] * 2,
        out_specs=pl.BlockSpec(memory_space=pl.ANY),
        scratch_shapes=[vm((4, 8, 8, 128), F32), vm((8, 4096), F32), vm((8, 4096), F32), dma((3, 4))],
        compiler_params=pltpu.CompilerParams(vmem_limit_bytes=56 * 1024 * 1024),
        name="mix",
    )(conv.reshape(8, 32, 128), query)


def solution(mesh):
    return jax.shard_map(
        local,
        mesh=mesh,
        in_specs=(
            P(None, ("seq", "ch")),
            P("ch", "seq"),
            P("ch", "seq"),
            P("ch", "seq"),
            P(None, "ch", None),
            P("ch"),
        ),
        out_specs=P(None, ("seq", "ch")),
        check_vma=False,
    )
```

```python
import functools

import jax
import jax.numpy as jnp
import ml_dtypes
import numpy as np
from jax import lax
from jax.experimental import pallas as pl
from jax.experimental.pallas import tpu as pltpu
from jax.sharding import PartitionSpec as P

MESH = pl.DeviceIdType.MESH
F32 = jnp.float32
BF16 = jnp.bfloat16


def two_parts(table):
    high = table.astype(np.float32).astype(ml_dtypes.bfloat16)
    low = (table - high.astype(np.float64)).astype(np.float32).astype(ml_dtypes.bfloat16)
    return high, low


def as_left(table):
    high, low = two_parts(table)
    return np.concatenate([high, high, low], axis=1)


def as_right(table):
    high, low = two_parts(table)
    return np.concatenate([high, high, low], axis=0)


FORWARD = (
    (((0, 0), (0, 1)), ((1, 0), (1, 1), (3, 0), (3, 1)), ((2, 0), (2, 1))),
    (((0, 1), (2, 1)), ((0, 0), (2, 0)), ((1, 0), (1, 1), (3, 0), (3, 1))),
)
BACK = ((0, 4), (1, 5), (2, 3, 6, 7))
BACK_START = [sum(len(q) for q in BACK[:p]) for p in range(len(BACK))]
PLANE = sorted(
    ((a, b, e) for a in range(4) for b in range(4) for e in range(2) if (a, b, e) != (0, 0, 0)),
    key=lambda p: (-(2 - abs(2 - p[0])) - (2 - abs(2 - p[1])), p),
)


NEAR = [p for p in PLANE if p[:2] in ((0, 0), (0, 1), (0, 3), (1, 0), (3, 0))]


def make_tables():
    j1, k1 = np.arange(32), np.arange(32)
    lanes = np.arange(128)
    head = 2 * np.pi * np.outer(k1 + 0.5, j1) / 64
    step = np.stack([np.cos(head), -np.sin(head)])
    head_in = [np.einsum("rkj,ab->rakbj", step, np.eye(n)).reshape(64 * n, 32 * n) for n in (2, 4)]
    head_out = [np.einsum("rkj,ab->bjrak", step, np.eye(n)).reshape(32 * n, 64 * n) for n in (2, 4)]
    angle = 2 * np.pi * np.outer(k1 + 0.5, lanes) / 8192
    turn = np.concatenate([np.cos(angle), np.sin(angle)], axis=1).astype(np.float32)
    turn = [np.tile(turn, (n, 1)) for n in (2, 4)]
    tail = 2 * np.pi * np.outer(lanes, lanes) / 128
    c, s = np.cos(tail), np.sin(tail)
    tail_in = np.block([[c, -s], [s, c]])
    tail_out = np.block([[c, s], [-s, c]])
    place = np.arange(256).reshape(4, 4, 8, 2).transpose(1, 3, 0, 2).reshape(256)
    nu = np.arange(256)
    phase = 2 * np.pi * np.outer(nu, place) / 512
    cosines, sines = np.cos(phase), np.sin(phase)
    sines[0] = np.cos(np.pi * place)
    block_in = np.concatenate([cosines, sines], axis=0)
    block_out = block_in.T.reshape(8, 32, 512)[[z for piece in BACK for z in piece]].reshape(256, 512) * 2.0**-21
    shift = np.stack([np.sin(2 * np.pi * nu / 512), np.cos(2 * np.pi * nu / 512), np.cos(2 * np.pi * nu / 512)])
    shift[2, 0] = -1.0
    shift = np.repeat(shift, 128, axis=0).T.astype(np.float32)
    return (
        as_left(head_in[0]),
        as_left(head_in[1]),
        as_right(tail_in),
        turn[0],
        turn[1],
        as_left(block_in),
        as_left(block_out),
        shift,
        as_right(tail_out),
        as_left(head_out[0]),
        as_left(head_out[1]),
    )


def put_split(ref, value, axis):
    high = value.astype(BF16)
    low = (value - high.astype(F32)).astype(BF16)
    n = value.shape[axis]
    for place, part in enumerate((high, low, high)):
        if axis == 0:
            ref[place * n : (place + 1) * n, :] = part
        else:
            ref[:, place * n : (place + 1) * n] = part


def mm(a, b):
    return jnp.dot(a, b, preferred_element_type=F32)


def kernel(
    key, value, filt, taps_h, bias_h,
    head_in2_h, head_in4_h, tail_in_h, turn2_h, turn4_h, block_in_h, block_out_h, shift_h, tail_out_h, head_out2_h, head_out4_h,
    out,
    key_v, value_v, filt_v, taps, bias,
    head_in2, head_in4, tail_in, turn2, turn4, block_in, block_out, shift, tail_out, head_out2, head_out4,
    gate, ends_s, ends_z, ends_r, starts, rows_f, rows_s, zbuf_f, zbuf_s, sbuf, rbuf, spec, back_s, back_r, done_s,
    right_a, left_b, right_q, right_i, left_o, right_o,
    load_sem, ends_send, ends_recv, z_send, z_recv, xy_send, xy_recv,
    back_send, back_recv, done_send, done_recv, widen,
):
    seq = lax.axis_index("seq")
    ch = lax.axis_index("ch")
    y = seq // 32
    zh = (seq // 8) % 4
    s = seq % 8
    me = y * 8 + s
    z = zh * 2 + ch
    zbuf = (zbuf_f, zbuf_s)
    rows = (rows_f, rows_s)

    in_y = [(y + a) % 4 for a in range(4)]
    in_x = [(s // 2 + b) % 4 * 2 for b in range(4)]
    in_core = [s % 2, 1 - s % 2]

    def plane_peers(places=PLANE):
        for a, b, e in places:
            at = in_x[b] + in_core[e]
            yield in_y[a] * 8 + at, {"seq": in_y[a] * 32 + zh * 8 + at, "ch": ch}

    def z_device(to):
        return {"seq": y * 32 + (to // 2) * 8 + s, "ch": to % 2}

    def tile(i, n=8):
        return pl.ds(pl.multiple_of(i * n, n), n)

    def total(ref, sem):
        return pltpu.make_async_copy(ref, ref, sem)

    barrier = pltpu.get_barrier_semaphore()

    @pl.loop(0, 7)
    def _(i):
        pl.semaphore_signal(
            barrier, inc=1, device_id=z_device((z + 1 + (i + 3) % 7) % 8), device_id_type=MESH
        )

    for _, peer in plane_peers(NEAR):
        pl.semaphore_signal(barrier, inc=1, device_id=peer, device_id_type=MESH)

    loads = [
        (filt, filt_v), (bias_h, bias), (key, key_v), (value, value_v), (taps_h, taps),
        (head_in4_h, head_in4), (turn4_h, turn4), (tail_in_h, tail_in),
        (block_in_h, block_in), (shift_h, shift), (block_out_h, block_out),
        (tail_out_h, tail_out), (turn2_h, turn2), (head_in2_h, head_in2), (head_out2_h, head_out2), (head_out4_h, head_out4),
    ]
    loads = [pltpu.make_async_copy(a, b, load_sem.at[i]) for i, (a, b) in enumerate(loads)]
    for load in loads:
        load.start()
    drains = []
    pend = {}
    (l_filt, l_bias, l_key, l_value, l_taps, l_hi, l_turn, l_ti, l_bi, l_sh, l_bo, l_to, l_t2, l_hi2, l_ho2, l_ho4) = loads

    l_filt.wait()
    l_bias.wait()
    for c in range(4):
        rows_f[c] = filt_v[pl.ds(c, 64, stride=4), :]
    first = jnp.where((lax.broadcasted_iota(jnp.int32, (1, 128), 1) == 0) & (seq == 0), 1.0, 0.0)
    for c in range(4):
        rows_f[c, 0:1, :] = rows_f[c, 0:1, :] + first * bias[c]

    l_key.wait()
    l_value.wait()
    l_taps.wait()
    for i, source in enumerate((key_v, value_v)):
        for c in range(4):
            ends_s[c, i : i + 1, :] = source[252 + c : 253 + c, :]
            ends_s[c, 2 + i : 3 + i, :] = source[c : c + 1, :]
    row = lax.broadcasted_iota(jnp.int32, (8, 128), 0) % 4
    lanes = lax.broadcasted_iota(jnp.int32, (256, 128), 1)

    def tap_rows(j, i):
        t = [taps[j, i, c] for c in range(4)]
        return jnp.where(row < 2, jnp.where(row == 0, t[0], t[1]), jnp.where(row == 2, t[2], t[3]))

    def short(source, i):
        x = source[...]
        result = None
        for j in range(3):
            t = tap_rows(j, i)
            moved = x
            if j > 0:
                near = pltpu.roll(x, j, 1)
                moved = jnp.where(lanes < j, pltpu.roll(near, 4, 0), near)
            term = t[None] * moved.reshape(32, 8, 128)
            result = term if result is None else result + term
        return result

    gate[...] = (short(key_v, 0) * short(value_v, 1)).reshape(256, 128)
    for c in range(4):
        rows_s[c] = gate[pl.ds(c, 64, stride=4), :]

    pl.semaphore_wait(barrier, 16)

    for i in (2, 3, 1):
        to = (zh + i) % 4
        pltpu.make_async_remote_copy(
            src_ref=ends_s.at[to],
            dst_ref=ends_z.at[zh],
            send_sem=ends_send.at[0],
            recv_sem=ends_recv.at[0],
            device_id=z_device(to * 2 + ch),
            device_id_type=MESH,
        ).start()
    drains.append(total(ends_s.at[0:3], ends_send.at[0]).wait)

    def z_exchange(f):
        for i in (2, 3, 1):
            to = (zh + i) % 4
            pltpu.make_async_remote_copy(
                src_ref=rows[f].at[to],
                dst_ref=zbuf[f].at[4 - i],
                send_sem=z_send.at[f],
                recv_sem=z_recv.at[f, 4 - i],
                device_id=z_device(to * 2 + ch),
                device_id_type=MESH,
            ).start()
            pend['z',f,4-i] = total(zbuf[f].at[4 - i], z_recv.at[f, 4 - i])
        drains.append(lambda: total(rows[f].at[0:3], z_send.at[f]).wait())

    z_exchange(0)
    z_exchange(1)
    for k in range(3):
        for _, peer in plane_peers(NEAR):
            pl.semaphore_signal(widen.at[k], inc=1, device_id=peer, device_id_type=MESH)
        pl.semaphore_wait(widen.at[k], 9)
    ends_z[zh] = ends_s[zh]
    total(ends_z.at[0:3], ends_recv.at[0]).wait()

    @pl.loop(0, 4)
    def _(block):
        after = (y * 32 + block * 8 + s + 1) % 128
        pltpu.make_async_remote_copy(
            src_ref=ends_z.at[block],
            dst_ref=ends_r.at[(after // 8) % 4],
            send_sem=ends_send.at[1],
            recv_sem=ends_recv.at[1],
            device_id={"seq": (after // 32) * 32 + zh * 8 + after % 8, "ch": ch},
            device_id_type=MESH,
        ).start()

    pend['e'] = total(ends_r, ends_recv.at[1])
    drains.append(total(ends_z, ends_send.at[1]).wait)

    def first_rows():
        pend.pop('e').wait()
        lane = lax.broadcasted_iota(jnp.int32, (4, 128), 1)
        origin = lax.broadcasted_iota(jnp.int32, (4, 128), 0) + me == 0

        def whole(i):
            x = jnp.concatenate([ends_z[b, 2 + i : 3 + i, :] for b in range(4)], axis=0)
            before = jnp.concatenate([ends_r[b, i : i + 1, :] for b in range(4)], axis=0)
            before = jnp.where(origin, 0.0, before)
            result = taps[0, i, zh] * x
            for j in (1, 2):
                moved = jnp.where(lane < j, pltpu.roll(before, j, 1), pltpu.roll(x, j, 1))
                result = result + taps[j, i, zh] * moved
            return result

        fixed = whole(0) * whole(1)
        for b in range(4):
            starts[b, 0:1, :] = fixed[b : b + 1, :]

    for f in range(2):
        zbuf[f][0] = rows[f][zh]

    def forward(f, p):
        which = FORWARD[f][p]
        count = len(which)
        head_in, turn = (head_in2, turn2) if count == 2 else (head_in4, turn4)
        for d, half in which:
            if ('z', f, d) in pend:
                pend.pop(('z',f,d)).wait()
            if f == 1 and half == 0:
                if 'e' in pend:
                    first_rows()
                zbuf_s[d, 0:1, :] = starts[(zh + d) % 4, 0:1, :]
        blocks = [zbuf[f][d, 32 * half : 32 * half + 32, :] for d, half in which]
        right = right_a.at[0 : 96 * count]
        put_split(right, jnp.concatenate(blocks, axis=0), 0)
        if f == 0 and p == 1:
            l_hi.wait()
            l_turn.wait()
        both = mm(head_in[...], right[...])
        real, imag = both[0 : 32 * count], both[32 * count : 64 * count]
        if f == 0 and p == 0:
            l_ti.wait()
        c, sn = turn[:, 0:128], turn[:, 128:256]
        turned = jnp.concatenate([real * c + imag * sn, imag * c - real * sn], axis=1)
        left = left_b.at[0 : 32 * count]
        put_split(left, turned, 1)
        spread = mm(left[...], tail_in[...])
        for b in range(count):
            for i in range(2):
                sbuf[f][p][:, 2 * b + i, :] = spread[32 * b : 32 * b + 32, 128 * i : 128 * i + 128]
        for d, peer in plane_peers():
            pltpu.make_async_remote_copy(
                src_ref=sbuf[f][p].at[d],
                dst_ref=rbuf[f][p].at[me],
                send_sem=xy_send.at[f, p],
                recv_sem=xy_recv.at[f, p],
                device_id=peer,
                device_id_type=MESH,
            ).start()
        rbuf[f][p][me] = sbuf[f][p][me]
        pend['x',f,p] = total(rbuf[f][p].at[0:31], xy_recv.at[f, p])
        drains.append(lambda: total(sbuf[f][p].at[0:31], xy_send.at[f, p]).wait())

    top_row = lax.broadcasted_iota(jnp.int32, (128, 128), 0) == 0
    sign = jnp.where(me % 2 == 0, 1.0, -1.0)

    def times(a, b):
        return a[0] * b[0] - a[1] * b[1], a[0] * b[1] + a[1] * b[0]

    def across(f):
        for p in range(len(FORWARD[f])):
            pend.pop(('x',f,p)).wait()
            for n, (d, half) in enumerate(FORWARD[f][p]):
                pair = [rbuf[f][p][:, 2 * n + i, :] for i in range(2)]
                pair = jnp.concatenate(pair, axis=1)
                high = pair.astype(BF16)
                low = (pair - high.astype(F32)).astype(BF16)
                base = (zh + d) % 4 * 64 + half * 32
                for k, part in enumerate((high, low, high)):
                    right_q[pl.ds(pl.multiple_of(base + 256 * k, 32), 32), :] = part
        if f == 0:
            l_bi.wait()
            l_sh.wait()
        for m in range(0, 256, 128):
            part = slice(m, m + 128)
            cosines = mm(block_in[part, :], right_q[...])
            sines = mm(block_in[256 + m : 384 + m, :], right_q[...])
            cre, cim, sre, sim = cosines[:, 0:128], cosines[:, 128:256], sines[:, 0:128], sines[:, 128:256]

            def alone(first, other):
                return jnp.where(top_row, first, other) if m == 0 else other

            up = alone(cre, cre + sim), alone(cim, cim - sre)
            down = alone(sre, cre - sim), alone(sim, cim + sre)
            if f == 0:
                tilt = sign * shift[part, 0:128]
                up = times(up, (1.0 + tilt, sign * shift[part, 128:256]))
                down = times(down, (1.0 - tilt, sign * shift[part, 256:384]))
                for k, x in enumerate(up + down):
                    spec[part, 128 * k : 128 * k + 128] = x
            else:
                up = times(up, (spec[part, 0:128], spec[part, 128:256]))
                down = times(down, (spec[part, 256:384], spec[part, 384:512]))
                even = [alone(up[k], up[k] + down[k]) for k in range(2)]
                odd = [alone(down[0], down[1] - up[1]), alone(down[1], up[0] - down[0])]
                for at, pair in ((m, even), (256 + m, odd)):
                    pair = jnp.concatenate(pair, axis=1)
                    high = pair.astype(BF16)
                    low = (pair - high.astype(F32)).astype(BF16)
                    for k, x in enumerate((high, low, high)):
                        right_i[512 * k + at : 512 * k + at + 128, :] = x

    l_t2.wait()
    l_hi2.wait()
    for f in range(2):
        for p in range(len(FORWARD[f])):
            forward(f, p)
    across(0)
    across(1)
    l_bo.wait()

    def send_back(p):
        low, count = 32 * BACK_START[p], len(BACK[p])
        both = mm(block_out[low : low + 32 * count, :], right_i[...])
        for n in range(count):
            for i in range(2):
                back_s[p][:, 2 * n + i, :] = both[32 * n : 32 * n + 32, 128 * i : 128 * i + 128]
        for d, peer in plane_peers():
            pltpu.make_async_remote_copy(
                src_ref=back_s[p].at[d],
                dst_ref=back_r[p].at[me],
                send_sem=back_send.at[p],
                recv_sem=back_recv.at[p],
                device_id=peer,
                device_id_type=MESH,
            ).start()
        back_r[p][me] = back_s[p][me]
        pend['b',p] = total(back_r[p].at[0:31], back_recv.at[p])
        drains.append(lambda: total(back_s[p].at[0:31], back_send.at[p]).wait())

    for p in range(len(BACK)):
        send_back(p)
    channel = ch * 4 + zh

    def finish_blocks(p):
        count = len(BACK[p])
        turn, head_out = (turn2, head_out2) if count == 2 else (turn4, head_out4)
        pend.pop(('b',p)).wait()
        high_low = []
        for i in range(2):
            for n in range(count):
                part = back_r[p][:, 2 * n + i, :]
                high = part.astype(BF16)
                low = (part - high.astype(F32)).astype(BF16)
                for k, piece in enumerate((high, low, high)):
                    left_o[32 * n : 32 * n + 32, 256 * k + 128 * i : 256 * k + 128 * i + 128] = piece
        if p == 0:
            l_to.wait()
            l_ho2.wait()
            l_ho4.wait()
        mixed = mm(left_o[0 : 32 * count, :], tail_out[...])
        c, sn = turn[:, 0:128], turn[:, 128:256]
        real, imag = mixed[:, 0:128], mixed[:, 128:256]
        right = right_o.at[0 : 192 * count]
        put_split(right, jnp.concatenate([real * c - imag * sn, real * sn + imag * c], axis=0), 0)
        low = 32 * BACK_START[p]
        done_s[low : low + 32 * count, :] = mm(head_out[...], right[...])
        for n, to in enumerate(BACK[p]):
            block = done_s.at[low + 32 * n : low + 32 * n + 32]

            @pl.when(to == z)
            def _():
                pltpu.make_async_copy(block, out.at[tile(channel, 32)], done_recv).start()

            @pl.when(to != z)
            def _():
                pltpu.make_async_remote_copy(
                    src_ref=block,
                    dst_ref=out.at[tile(channel, 32)],
                    send_sem=done_send,
                    recv_sem=done_recv,
                    device_id=z_device(to),
                    device_id_type=MESH,
                ).start()

    for p in range(len(BACK)):
        finish_blocks(p)
    total(out, done_recv).wait()
    total(done_s.at[0:224], done_send).wait()
    for drain in drains:
        drain()


def mix(conv, query, out, conv_v, query_v, out_v, sem):
    loads, stores = [], []
    for k in range(4):
        lanes = pl.ds(1024 * k, 1024)
        loads.append((
            pltpu.make_async_copy(conv.at[:, 8 * k : 8 * k + 8], conv_v.at[k], sem.at[0, k]),
            pltpu.make_async_copy(query.at[:, lanes], query_v.at[:, lanes], sem.at[1, k]),
        ))
        stores.append(pltpu.make_async_copy(out_v.at[:, lanes], out.at[:, lanes], sem.at[2, k]))
        for load in loads[k]:
            load.start()
    for k in range(4):
        for load in loads[k]:
            load.wait()
        for j in range(8):
            lanes = slice(1024 * k + 128 * j, 1024 * k + 128 * j + 128)
            out_v[:, lanes] = conv_v[k, :, j, :] * query_v[:, lanes]
        stores[k].start()
    for store in stores:
        store.wait()


def by_time(x):
    return x.reshape(4, 64, 128).transpose(1, 0, 2).reshape(256, 128)


def local(query, key, value, filters, short_taps, bias):
    tables = make_tables()
    vm = pltpu.VMEM
    dma = pltpu.SemaphoreType.DMA
    table_scratch = [vm(t.shape, t.dtype) for t in tables]
    conv = pl.pallas_call(
        kernel,
        out_shape=jax.ShapeDtypeStruct((256, 128), F32),
        in_specs=[pl.BlockSpec(memory_space=pl.ANY)] * 16,
        out_specs=pl.BlockSpec(memory_space=pl.ANY),
        scratch_shapes=[vm((256, 128), F32)] * 3
        + [pltpu.SMEM((3, 2, 4), F32), pltpu.SMEM((4,), F32)]
        + table_scratch
        + [
            vm((256, 128), F32),
            vm((4, 8, 128), F32),
            vm((4, 8, 128), F32),
            vm((4, 8, 128), F32),
            vm((4, 8, 128), F32),
            vm((4, 64, 128), F32),
            vm((4, 64, 128), F32),
            vm((4, 64, 128), F32),
            vm((4, 64, 128), F32),
            [[vm((32, 2 * len(p), 128), F32) for p in pieces] for pieces in FORWARD],
            [[vm((32, 2 * len(p), 128), F32) for p in pieces] for pieces in FORWARD],
            vm((256, 512), F32),
            [vm((32, 2 * len(p), 128), F32) for p in BACK],
            [vm((32, 2 * len(p), 128), F32) for p in BACK],
            vm((256, 128), F32),
            vm((384, 128), BF16),
            vm((128, 768), BF16),
            vm((768, 256), BF16),
            vm((1536, 256), BF16),
            vm((128, 768), BF16),
            vm((768, 128), BF16),
            dma((16,)),
            dma((2,)), dma((2,)),
            dma((2,)), dma((2, 4)),
            dma((2, 3)), dma((2, 3)),
            dma((len(BACK),)), dma((len(BACK),)),
            dma(()), dma(()),
            pltpu.SemaphoreType.REGULAR((3,)),
        ],
        compiler_params=pltpu.CompilerParams(
            collective_id=0, has_side_effects=True, vmem_limit_bytes=56 * 1024 * 1024
        ),
        name="long_convolution",
    )(
        by_time(key), by_time(value), by_time(filters), short_taps.transpose(2, 0, 1), bias,
        *[jnp.asarray(t) for t in tables],
    )
    return pl.pallas_call(
        mix,
        out_shape=jax.ShapeDtypeStruct((8, 4096), F32),
        in_specs=[pl.BlockSpec(memory_space=pl.ANY)] * 2,
        out_specs=pl.BlockSpec(memory_space=pl.ANY),
        scratch_shapes=[vm((4, 8, 8, 128), F32), vm((8, 4096), F32), vm((8, 4096), F32), dma((3, 4))],
        compiler_params=pltpu.CompilerParams(vmem_limit_bytes=56 * 1024 * 1024),
        name="mix",
    )(conv.reshape(8, 32, 128), query)


def solution(mesh):
    return jax.shard_map(
        local,
        mesh=mesh,
        in_specs=(
            P(None, ("seq", "ch")),
            P("ch", "seq"),
            P("ch", "seq"),
            P("ch", "seq"),
            P(None, "ch", None),
            P("ch"),
        ),
        out_specs=P(None, ("seq", "ch")),
        check_vma=False,
    )
```

```python
import functools

import jax
import jax.numpy as jnp
import ml_dtypes
import numpy as np
from jax import lax
from jax.experimental import pallas as pl
from jax.experimental.pallas import tpu as pltpu
from jax.sharding import PartitionSpec as P

MESH = pl.DeviceIdType.MESH
F32 = jnp.float32
BF16 = jnp.bfloat16


def two_parts(table):
    high = table.astype(np.float32).astype(ml_dtypes.bfloat16)
    low = (table - high.astype(np.float64)).astype(np.float32).astype(ml_dtypes.bfloat16)
    return high, low


def as_left(table):
    high, low = two_parts(table)
    return np.concatenate([high, high, low], axis=1)


def as_right(table):
    high, low = two_parts(table)
    return np.concatenate([high, high, low], axis=0)


FORWARD = (
    (((0, 0), (0, 1)), ((1, 0), (1, 1), (3, 0), (3, 1)), ((2, 0), (2, 1))),
    (((0, 1), (2, 1)), ((0, 0), (2, 0)), ((1, 0), (1, 1), (3, 0), (3, 1))),
)
BACK = ((0, 4), (1, 5), (2, 3, 6, 7))
BACK_START = [sum(len(q) for q in BACK[:p]) for p in range(len(BACK))]
PLANE = sorted(
    ((a, b, e) for a in range(4) for b in range(4) for e in range(2) if (a, b, e) != (0, 0, 0)),
    key=lambda p: (-(2 - abs(2 - p[0])) - (2 - abs(2 - p[1])), p),
)


NEAR = [p for p in PLANE if p[:2] in ((0, 0), (0, 1), (0, 3), (1, 0), (3, 0))]


def make_tables():
    j1, k1 = np.arange(32), np.arange(32)
    lanes = np.arange(128)
    head = 2 * np.pi * np.outer(k1 + 0.5, j1) / 64
    step = np.stack([np.cos(head), -np.sin(head)])
    head_in = [np.einsum("rkj,ab->rakbj", step, np.eye(n)).reshape(64 * n, 32 * n) for n in (2, 4)]
    head_out = [np.einsum("rkj,ab->bjrak", step, np.eye(n)).reshape(32 * n, 64 * n) for n in (2, 4)]
    angle = 2 * np.pi * np.outer(k1 + 0.5, lanes) / 8192
    turn = np.concatenate([np.cos(angle), np.sin(angle)], axis=1).astype(np.float32)
    turn = [np.tile(turn, (n, 1)) for n in (2, 4)]
    tail = 2 * np.pi * np.outer(lanes, lanes) / 128
    c, s = np.cos(tail), np.sin(tail)
    tail_in = np.block([[c, -s], [s, c]])
    tail_out = np.block([[c, s], [-s, c]])
    place = np.arange(256).reshape(4, 4, 8, 2).transpose(1, 3, 0, 2).reshape(256)
    nu = np.arange(256)
    phase = 2 * np.pi * np.outer(nu, place) / 512
    cosines, sines = np.cos(phase), np.sin(phase)
    sines[0] = np.cos(np.pi * place)
    block_in = np.concatenate([cosines, sines], axis=0)
    block_out = block_in.T.reshape(8, 32, 512)[[z for piece in BACK for z in piece]].reshape(256, 512) * 2.0**-21
    shift = np.stack([np.sin(2 * np.pi * nu / 512), np.cos(2 * np.pi * nu / 512), np.cos(2 * np.pi * nu / 512)])
    shift[2, 0] = -1.0
    shift = np.repeat(shift, 128, axis=0).T.astype(np.float32)
    return (
        as_left(head_in[0]),
        as_left(head_in[1]),
        as_right(tail_in),
        turn[0],
        turn[1],
        as_left(block_in),
        as_left(block_out),
        shift,
        as_right(tail_out),
        as_left(head_out[0]),
        as_left(head_out[1]),
    )


def put_split(ref, value, axis):
    high = value.astype(BF16)
    low = (value - high.astype(F32)).astype(BF16)
    n = value.shape[axis]
    for place, part in enumerate((high, low, high)):
        if axis == 0:
            ref[place * n : (place + 1) * n, :] = part
        else:
            ref[:, place * n : (place + 1) * n] = part


def mm(a, b):
    return jnp.dot(a, b, preferred_element_type=F32)


def kernel(
    key, value, filt, taps_h, bias_h,
    head_in2_h, head_in4_h, tail_in_h, turn2_h, turn4_h, block_in_h, block_out_h, shift_h, tail_out_h, head_out2_h, head_out4_h,
    out,
    key_v, value_v, filt_v, taps, bias,
    head_in2, head_in4, tail_in, turn2, turn4, block_in, block_out, shift, tail_out, head_out2, head_out4,
    gate, ends_s, ends_z, ends_r, starts, rows_f, rows_s, zbuf_f, zbuf_s, sbuf, rbuf, spec, back_s, back_r, done_s,
    right_a, left_b, right_q, right_i, left_o, right_o,
    load_sem, ends_send, ends_recv, z_send, z_recv, xy_send, xy_recv,
    back_send, back_recv, done_send, done_recv, widen,
):
    seq = lax.axis_index("seq")
    ch = lax.axis_index("ch")
    y = seq // 32
    zh = (seq // 8) % 4
    s = seq % 8
    me = y * 8 + s
    z = zh * 2 + ch
    zbuf = (zbuf_f, zbuf_s)
    rows = (rows_f, rows_s)

    in_y = [(y + a) % 4 for a in range(4)]
    in_x = [(s // 2 + b) % 4 * 2 for b in range(4)]
    in_core = [s % 2, 1 - s % 2]

    def plane_peers(places=PLANE):
        for a, b, e in places:
            at = in_x[b] + in_core[e]
            yield in_y[a] * 8 + at, {"seq": in_y[a] * 32 + zh * 8 + at, "ch": ch}

    def z_device(to):
        return {"seq": y * 32 + (to // 2) * 8 + s, "ch": to % 2}

    def tile(i, n=8):
        return pl.ds(pl.multiple_of(i * n, n), n)

    def total(ref, sem):
        return pltpu.make_async_copy(ref, ref, sem)

    barrier = pltpu.get_barrier_semaphore()

    @pl.loop(0, 7)
    def _(i):
        pl.semaphore_signal(
            barrier, inc=1, device_id=z_device((z + 1 + (i + 3) % 7) % 8), device_id_type=MESH
        )

    for _, peer in plane_peers(NEAR):
        pl.semaphore_signal(barrier, inc=1, device_id=peer, device_id_type=MESH)

    loads = [
        (filt, filt_v), (bias_h, bias), (key, key_v), (value, value_v), (taps_h, taps),
        (head_in4_h, head_in4), (turn4_h, turn4), (tail_in_h, tail_in),
        (block_in_h, block_in), (shift_h, shift), (block_out_h, block_out),
        (tail_out_h, tail_out), (turn2_h, turn2), (head_in2_h, head_in2), (head_out2_h, head_out2), (head_out4_h, head_out4),
    ]
    loads = [pltpu.make_async_copy(a, b, load_sem.at[i]) for i, (a, b) in enumerate(loads)]
    for load in loads:
        load.start()
    drains = []
    pend = {}
    (l_filt, l_bias, l_key, l_value, l_taps, l_hi, l_turn, l_ti, l_bi, l_sh, l_bo, l_to, l_t2, l_hi2, l_ho2, l_ho4) = loads

    l_filt.wait()
    l_bias.wait()
    for c in range(4):
        rows_f[c] = filt_v[pl.ds(c, 64, stride=4), :]
    first = jnp.where((lax.broadcasted_iota(jnp.int32, (1, 128), 1) == 0) & (seq == 0), 1.0, 0.0)
    for c in range(4):
        rows_f[c, 0:1, :] = rows_f[c, 0:1, :] + first * bias[c]

    l_key.wait()
    l_value.wait()
    l_taps.wait()
    for i, source in enumerate((key_v, value_v)):
        for c in range(4):
            ends_s[c, i : i + 1, :] = source[252 + c : 253 + c, :]
            ends_s[c, 2 + i : 3 + i, :] = source[c : c + 1, :]
    row = lax.broadcasted_iota(jnp.int32, (8, 128), 0) % 4
    lanes = lax.broadcasted_iota(jnp.int32, (256, 128), 1)

    def tap_rows(j, i):
        t = [taps[j, i, c] for c in range(4)]
        return jnp.where(row < 2, jnp.where(row == 0, t[0], t[1]), jnp.where(row == 2, t[2], t[3]))

    def short(source, i):
        x = source[...]
        result = None
        for j in range(3):
            t = tap_rows(j, i)
            moved = x
            if j > 0:
                near = pltpu.roll(x, j, 1)
                moved = jnp.where(lanes < j, pltpu.roll(near, 4, 0), near)
            term = t[None] * moved.reshape(32, 8, 128)
            result = term if result is None else result + term
        return result

    gate[...] = (short(key_v, 0) * short(value_v, 1)).reshape(256, 128)
    for c in range(4):
        rows_s[c] = gate[pl.ds(c, 64, stride=4), :]

    pl.semaphore_wait(barrier, 16)

    for i in (2, 3, 1):
        to = (zh + i) % 4
        pltpu.make_async_remote_copy(
            src_ref=ends_s.at[to],
            dst_ref=ends_z.at[zh],
            send_sem=ends_send.at[0],
            recv_sem=ends_recv.at[0],
            device_id=z_device(to * 2 + ch),
            device_id_type=MESH,
        ).start()
    drains.append(total(ends_s.at[0:3], ends_send.at[0]).wait)

    def z_exchange(f):
        for i in (2, 3, 1):
            to = (zh + i) % 4
            pltpu.make_async_remote_copy(
                src_ref=rows[f].at[to],
                dst_ref=zbuf[f].at[4 - i],
                send_sem=z_send.at[f],
                recv_sem=z_recv.at[f, 4 - i],
                device_id=z_device(to * 2 + ch),
                device_id_type=MESH,
            ).start()
            pend['z',f,4-i] = total(zbuf[f].at[4 - i], z_recv.at[f, 4 - i])
        drains.append(lambda: total(rows[f].at[0:3], z_send.at[f]).wait())

    z_exchange(0)
    z_exchange(1)
    for k in range(3):
        for _, peer in plane_peers(NEAR):
            pl.semaphore_signal(widen.at[k], inc=1, device_id=peer, device_id_type=MESH)
        pl.semaphore_wait(widen.at[k], 9)
    ends_z[zh] = ends_s[zh]
    total(ends_z.at[0:3], ends_recv.at[0]).wait()

    @pl.loop(0, 4)
    def _(block):
        after = (y * 32 + block * 8 + s + 1) % 128
        pltpu.make_async_remote_copy(
            src_ref=ends_z.at[block],
            dst_ref=ends_r.at[(after // 8) % 4],
            send_sem=ends_send.at[1],
            recv_sem=ends_recv.at[1],
            device_id={"seq": (after // 32) * 32 + zh * 8 + after % 8, "ch": ch},
            device_id_type=MESH,
        ).start()

    pend['e'] = total(ends_r, ends_recv.at[1])
    drains.append(total(ends_z, ends_send.at[1]).wait)

    def first_rows():
        pend.pop('e').wait()
        lane = lax.broadcasted_iota(jnp.int32, (4, 128), 1)
        origin = lax.broadcasted_iota(jnp.int32, (4, 128), 0) + me == 0

        def whole(i):
            x = jnp.concatenate([ends_z[b, 2 + i : 3 + i, :] for b in range(4)], axis=0)
            before = jnp.concatenate([ends_r[b, i : i + 1, :] for b in range(4)], axis=0)
            before = jnp.where(origin, 0.0, before)
            result = taps[0, i, zh] * x
            for j in (1, 2):
                moved = jnp.where(lane < j, pltpu.roll(before, j, 1), pltpu.roll(x, j, 1))
                result = result + taps[j, i, zh] * moved
            return result

        fixed = whole(0) * whole(1)
        for b in range(4):
            starts[b, 0:1, :] = fixed[b : b + 1, :]

    for f in range(2):
        zbuf[f][0] = rows[f][zh]

    def forward(f, p):
        which = FORWARD[f][p]
        count = len(which)
        head_in, turn = (head_in2, turn2) if count == 2 else (head_in4, turn4)
        for d, half in which:
            if ('z', f, d) in pend:
                pend.pop(('z',f,d)).wait()
            if f == 1 and half == 0:
                if 'e' in pend:
                    first_rows()
                zbuf_s[d, 0:1, :] = starts[(zh + d) % 4, 0:1, :]
        blocks = [zbuf[f][d, 32 * half : 32 * half + 32, :] for d, half in which]
        right = right_a.at[0 : 96 * count]
        put_split(right, jnp.concatenate(blocks, axis=0), 0)
        if f == 0 and p == 1:
            l_hi.wait()
            l_turn.wait()
        both = mm(head_in[...], right[...])
        real, imag = both[0 : 32 * count], both[32 * count : 64 * count]
        if f == 0 and p == 0:
            l_ti.wait()
        c, sn = turn[:, 0:128], turn[:, 128:256]
        turned = jnp.concatenate([real * c + imag * sn, imag * c - real * sn], axis=1)
        left = left_b.at[0 : 32 * count]
        put_split(left, turned, 1)
        spread = mm(left[...], tail_in[...])
        for b in range(count):
            for i in range(2):
                sbuf[f][p][:, 2 * b + i, :] = spread[32 * b : 32 * b + 32, 128 * i : 128 * i + 128]
        for d, peer in plane_peers():
            pltpu.make_async_remote_copy(
                src_ref=sbuf[f][p].at[d],
                dst_ref=rbuf[f][p].at[me],
                send_sem=xy_send.at[f, p],
                recv_sem=xy_recv.at[f, p],
                device_id=peer,
                device_id_type=MESH,
            ).start()
        rbuf[f][p][me] = sbuf[f][p][me]
        pend['x',f,p] = total(rbuf[f][p].at[0:31], xy_recv.at[f, p])
        drains.append(lambda: total(sbuf[f][p].at[0:31], xy_send.at[f, p]).wait())

    top_row = lax.broadcasted_iota(jnp.int32, (128, 128), 0) == 0
    sign = jnp.where(me % 2 == 0, 1.0, -1.0)

    def times(a, b):
        return a[0] * b[0] - a[1] * b[1], a[0] * b[1] + a[1] * b[0]

    def across(f):
        for p in range(len(FORWARD[f])):
            pend.pop(('x',f,p)).wait()
            for n, (d, half) in enumerate(FORWARD[f][p]):
                pair = [rbuf[f][p][:, 2 * n + i, :] for i in range(2)]
                pair = jnp.concatenate(pair, axis=1)
                high = pair.astype(BF16)
                low = (pair - high.astype(F32)).astype(BF16)
                base = (zh + d) % 4 * 64 + half * 32
                for k, part in enumerate((high, low, high)):
                    right_q[pl.ds(pl.multiple_of(base + 256 * k, 32), 32), :] = part
        if f == 0:
            l_bi.wait()
            l_sh.wait()
        for m in range(0, 256, 128):
            part = slice(m, m + 128)
            cosines = mm(block_in[part, :], right_q[...])
            sines = mm(block_in[256 + m : 384 + m, :], right_q[...])
            cre, cim, sre, sim = cosines[:, 0:128], cosines[:, 128:256], sines[:, 0:128], sines[:, 128:256]

            def alone(first, other):
                return jnp.where(top_row, first, other) if m == 0 else other

            up = alone(cre, cre + sim), alone(cim, cim - sre)
            down = alone(sre, cre - sim), alone(sim, cim + sre)
            if f == 0:
                tilt = sign * shift[part, 0:128]
                up = times(up, (1.0 + tilt, sign * shift[part, 128:256]))
                down = times(down, (1.0 - tilt, sign * shift[part, 256:384]))
                for k, x in enumerate(up + down):
                    spec[part, 128 * k : 128 * k + 128] = x
            else:
                up = times(up, (spec[part, 0:128], spec[part, 128:256]))
                down = times(down, (spec[part, 256:384], spec[part, 384:512]))
                even = [alone(up[k], up[k] + down[k]) for k in range(2)]
                odd = [alone(down[0], down[1] - up[1]), alone(down[1], up[0] - down[0])]
                for at, pair in ((m, even), (256 + m, odd)):
                    pair = jnp.concatenate(pair, axis=1)
                    high = pair.astype(BF16)
                    low = (pair - high.astype(F32)).astype(BF16)
                    for k, x in enumerate((high, low, high)):
                        right_i[512 * k + at : 512 * k + at + 128, :] = x

    l_t2.wait()
    l_hi2.wait()
    for f in range(2):
        for p in range(len(FORWARD[f])):
            forward(f, p)
    across(0)
    across(1)
    l_bo.wait()

    def send_back(p):
        low, count = 32 * BACK_START[p], len(BACK[p])
        both = mm(block_out[low : low + 32 * count, :], right_i[...])
        for n in range(count):
            for i in range(2):
                back_s[p][:, 2 * n + i, :] = both[32 * n : 32 * n + 32, 128 * i : 128 * i + 128]
        for d, peer in plane_peers():
            pltpu.make_async_remote_copy(
                src_ref=back_s[p].at[d],
                dst_ref=back_r[p].at[me],
                send_sem=back_send.at[p],
                recv_sem=back_recv.at[p],
                device_id=peer,
                device_id_type=MESH,
            ).start()
        back_r[p][me] = back_s[p][me]
        pend['b',p] = total(back_r[p].at[0:31], back_recv.at[p])
        drains.append(lambda: total(back_s[p].at[0:31], back_send.at[p]).wait())

    for p in range(len(BACK)):
        send_back(p)
    channel = ch * 4 + zh

    def finish_blocks(p):
        count = len(BACK[p])
        turn, head_out = (turn2, head_out2) if count == 2 else (turn4, head_out4)
        pend.pop(('b',p)).wait()
        high_low = []
        for i in range(2):
            for n in range(count):
                part = back_r[p][:, 2 * n + i, :]
                high = part.astype(BF16)
                low = (part - high.astype(F32)).astype(BF16)
                for k, piece in enumerate((high, low, high)):
                    left_o[32 * n : 32 * n + 32, 256 * k + 128 * i : 256 * k + 128 * i + 128] = piece
        if p == 0:
            l_to.wait()
            l_ho2.wait()
            l_ho4.wait()
        mixed = mm(left_o[0 : 32 * count, :], tail_out[...])
        c, sn = turn[:, 0:128], turn[:, 128:256]
        real, imag = mixed[:, 0:128], mixed[:, 128:256]
        right = right_o.at[0 : 192 * count]
        put_split(right, jnp.concatenate([real * c - imag * sn, real * sn + imag * c], axis=0), 0)
        low = 32 * BACK_START[p]
        done_s[low : low + 32 * count, :] = mm(head_out[...], right[...])
        for n, to in enumerate(BACK[p]):
            block = done_s.at[low + 32 * n : low + 32 * n + 32]

            @pl.when(to == z)
            def _():
                pltpu.make_async_copy(block, out.at[tile(channel, 32)], done_recv).start()

            @pl.when(to != z)
            def _():
                pltpu.make_async_remote_copy(
                    src_ref=block,
                    dst_ref=out.at[tile(channel, 32)],
                    send_sem=done_send,
                    recv_sem=done_recv,
                    device_id=z_device(to),
                    device_id_type=MESH,
                ).start()

    for p in range(len(BACK)):
        finish_blocks(p)
    for drain in drains:
        drain()
    total(done_s.at[0:224], done_send).wait()
    total(out, done_recv).wait()


def mix(conv, query, out, conv_v, query_v, out_v, sem):
    loads, stores = [], []
    for k in range(4):
        lanes = pl.ds(1024 * k, 1024)
        loads.append((
            pltpu.make_async_copy(conv.at[:, 8 * k : 8 * k + 8], conv_v.at[k], sem.at[0, k]),
            pltpu.make_async_copy(query.at[:, lanes], query_v.at[:, lanes], sem.at[1, k]),
        ))
        stores.append(pltpu.make_async_copy(out_v.at[:, lanes], out.at[:, lanes], sem.at[2, k]))
        for load in loads[k]:
            load.start()
    for k in range(4):
        for load in loads[k]:
            load.wait()
        for j in range(8):
            lanes = slice(1024 * k + 128 * j, 1024 * k + 128 * j + 128)
            out_v[:, lanes] = conv_v[k, :, j, :] * query_v[:, lanes]
        stores[k].start()
    for store in stores:
        store.wait()


def by_time(x):
    return x.reshape(4, 64, 128).transpose(1, 0, 2).reshape(256, 128)


def local(query, key, value, filters, short_taps, bias):
    tables = make_tables()
    vm = pltpu.VMEM
    dma = pltpu.SemaphoreType.DMA
    table_scratch = [vm(t.shape, t.dtype) for t in tables]
    conv = pl.pallas_call(
        kernel,
        out_shape=jax.ShapeDtypeStruct((256, 128), F32),
        in_specs=[pl.BlockSpec(memory_space=pl.ANY)] * 16,
        out_specs=pl.BlockSpec(memory_space=pl.ANY),
        scratch_shapes=[vm((256, 128), F32)] * 3
        + [pltpu.SMEM((3, 2, 4), F32), pltpu.SMEM((4,), F32)]
        + table_scratch
        + [
            vm((256, 128), F32),
            vm((4, 8, 128), F32),
            vm((4, 8, 128), F32),
            vm((4, 8, 128), F32),
            vm((4, 8, 128), F32),
            vm((4, 64, 128), F32),
            vm((4, 64, 128), F32),
            vm((4, 64, 128), F32),
            vm((4, 64, 128), F32),
            [[vm((32, 2 * len(p), 128), F32) for p in pieces] for pieces in FORWARD],
            [[vm((32, 2 * len(p), 128), F32) for p in pieces] for pieces in FORWARD],
            vm((256, 512), F32),
            [vm((32, 2 * len(p), 128), F32) for p in BACK],
            [vm((32, 2 * len(p), 128), F32) for p in BACK],
            vm((256, 128), F32),
            vm((384, 128), BF16),
            vm((128, 768), BF16),
            vm((768, 256), BF16),
            vm((1536, 256), BF16),
            vm((128, 768), BF16),
            vm((768, 128), BF16),
            dma((16,)),
            dma((2,)), dma((2,)),
            dma((2,)), dma((2, 4)),
            dma((2, 3)), dma((2, 3)),
            dma((len(BACK),)), dma((len(BACK),)),
            dma(()), dma(()),
            pltpu.SemaphoreType.REGULAR((3,)),
        ],
        compiler_params=pltpu.CompilerParams(
            collective_id=0, has_side_effects=True, vmem_limit_bytes=56 * 1024 * 1024
        ),
        name="long_convolution",
    )(
        by_time(key), by_time(value), by_time(filters), short_taps.transpose(2, 0, 1), bias,
        *[jnp.asarray(t) for t in tables],
    )
    return pl.pallas_call(
        mix,
        out_shape=jax.ShapeDtypeStruct((8, 4096), F32),
        in_specs=[pl.BlockSpec(memory_space=pl.ANY)] * 2,
        out_specs=pl.BlockSpec(memory_space=pl.ANY),
        scratch_shapes=[vm((4, 8, 8, 128), F32), vm((8, 4096), F32), vm((8, 4096), F32), dma((3, 4))],
        compiler_params=pltpu.CompilerParams(vmem_limit_bytes=56 * 1024 * 1024),
        name="mix",
    )(conv.reshape(8, 32, 128), query)


def solution(mesh):
    return jax.shard_map(
        local,
        mesh=mesh,
        in_specs=(
            P(None, ("seq", "ch")),
            P("ch", "seq"),
            P("ch", "seq"),
            P("ch", "seq"),
            P(None, "ch", None),
            P("ch"),
        ),
        out_specs=P(None, ("seq", "ch")),
        check_vma=False,
    )
```

```python
import functools

import jax
import jax.numpy as jnp
import ml_dtypes
import numpy as np
from jax import lax
from jax.experimental import pallas as pl
from jax.experimental.pallas import tpu as pltpu
from jax.sharding import PartitionSpec as P

MESH = pl.DeviceIdType.MESH
F32 = jnp.float32
BF16 = jnp.bfloat16


def two_parts(table):
    high = table.astype(np.float32).astype(ml_dtypes.bfloat16)
    low = (table - high.astype(np.float64)).astype(np.float32).astype(ml_dtypes.bfloat16)
    return high, low


def as_left(table):
    high, low = two_parts(table)
    return np.concatenate([high, high, low], axis=1)


def as_right(table):
    high, low = two_parts(table)
    return np.concatenate([high, high, low], axis=0)


FORWARD = (
    (((0, 0), (0, 1)), ((1, 0), (1, 1), (3, 0), (3, 1)), ((2, 0), (2, 1))),
    (((0, 1), (2, 1)), ((0, 0), (2, 0)), ((1, 0), (1, 1), (3, 0), (3, 1))),
)
BACK = ((0, 4), (1, 5), (2, 3, 6, 7))
BACK_START = [sum(len(q) for q in BACK[:p]) for p in range(len(BACK))]
PLANE = sorted(
    ((a, b, e) for a in range(4) for b in range(4) for e in range(2) if (a, b, e) != (0, 0, 0)),
    key=lambda p: (-(2 - abs(2 - p[0])) - (2 - abs(2 - p[1])), p),
)


NEAR = [p for p in PLANE if p[:2] in ((0, 0), (0, 1), (0, 3), (1, 0), (3, 0))]


def make_tables():
    j1, k1 = np.arange(32), np.arange(32)
    lanes = np.arange(128)
    head = 2 * np.pi * np.outer(k1 + 0.5, j1) / 64
    step = np.stack([np.cos(head), -np.sin(head)])
    head_in = [np.einsum("rkj,ab->rakbj", step, np.eye(n)).reshape(64 * n, 32 * n) for n in (2, 4)]
    head_out = [np.einsum("rkj,ab->bjrak", step, np.eye(n)).reshape(32 * n, 64 * n) for n in (2, 4)]
    angle = 2 * np.pi * np.outer(k1 + 0.5, lanes) / 8192
    turn = np.concatenate([np.cos(angle), np.sin(angle)], axis=1).astype(np.float32)
    turn = [np.tile(turn, (n, 1)) for n in (2, 4)]
    tail = 2 * np.pi * np.outer(lanes, lanes) / 128
    c, s = np.cos(tail), np.sin(tail)
    tail_in = np.block([[c, -s], [s, c]])
    tail_out = np.block([[c, s], [-s, c]])
    place = np.arange(256).reshape(4, 4, 8, 2).transpose(1, 3, 0, 2).reshape(256)
    nu = np.arange(256)
    phase = 2 * np.pi * np.outer(nu, place) / 512
    cosines, sines = np.cos(phase), np.sin(phase)
    sines[0] = np.cos(np.pi * place)
    block_in = np.concatenate([cosines, sines], axis=0)
    block_out = block_in.T.reshape(8, 32, 512)[[z for piece in BACK for z in piece]].reshape(256, 512) * 2.0**-21
    shift = np.stack([np.sin(2 * np.pi * nu / 512), np.cos(2 * np.pi * nu / 512), np.cos(2 * np.pi * nu / 512)])
    shift[2, 0] = -1.0
    shift = np.repeat(shift, 128, axis=0).T.astype(np.float32)
    return (
        as_left(head_in[0]),
        as_left(head_in[1]),
        as_right(tail_in),
        turn[0],
        turn[1],
        as_left(block_in),
        as_left(block_out),
        shift,
        as_right(tail_out),
        as_left(head_out[0]),
        as_left(head_out[1]),
    )


def put_split(ref, value, axis):
    high = value.astype(BF16)
    low = (value - high.astype(F32)).astype(BF16)
    n = value.shape[axis]
    for place, part in enumerate((high, low, high)):
        if axis == 0:
            ref[place * n : (place + 1) * n, :] = part
        else:
            ref[:, place * n : (place + 1) * n] = part


def mm(a, b):
    return jnp.dot(a, b, preferred_element_type=F32)


def kernel(
    key, value, filt, taps_h, bias_h,
    head_in2_h, head_in4_h, tail_in_h, turn2_h, turn4_h, block_in_h, block_out_h, shift_h, tail_out_h, head_out2_h, head_out4_h,
    out,
    key_v, value_v, filt_v, taps, bias,
    head_in2, head_in4, tail_in, turn2, turn4, block_in, block_out, shift, tail_out, head_out2, head_out4,
    gate, ends_s, ends_z, ends_r, starts, rows_f, rows_s, zbuf_f, zbuf_s, sbuf, rbuf, spec, back_s, back_r, done_s,
    right_a, left_b, right_q, right_i, left_o, right_o,
    load_sem, ends_send, ends_recv, z_send, z_recv, xy_send, xy_recv,
    back_send, back_recv, done_send, done_recv, widen,
):
    seq = lax.axis_index("seq")
    ch = lax.axis_index("ch")
    y = seq // 32
    zh = (seq // 8) % 4
    s = seq % 8
    me = y * 8 + s
    z = zh * 2 + ch
    zbuf = (zbuf_f, zbuf_s)
    rows = (rows_f, rows_s)

    in_y = [(y + a) % 4 for a in range(4)]
    in_x = [(s // 2 + b) % 4 * 2 for b in range(4)]
    in_core = [s % 2, 1 - s % 2]

    def plane_peers(places=PLANE):
        for a, b, e in places:
            at = in_x[b] + in_core[e]
            yield in_y[a] * 8 + at, {"seq": in_y[a] * 32 + zh * 8 + at, "ch": ch}

    def z_device(to):
        return {"seq": y * 32 + (to // 2) * 8 + s, "ch": to % 2}

    def tile(i, n=8):
        return pl.ds(pl.multiple_of(i * n, n), n)

    def total(ref, sem):
        return pltpu.make_async_copy(ref, ref, sem)

    barrier = pltpu.get_barrier_semaphore()

    @pl.loop(0, 7)
    def _(i):
        pl.semaphore_signal(
            barrier, inc=1, device_id=z_device((z + 1 + (i + 3) % 7) % 8), device_id_type=MESH
        )

    for _, peer in plane_peers(NEAR):
        pl.semaphore_signal(barrier, inc=1, device_id=peer, device_id_type=MESH)

    loads = [
        (filt, filt_v), (bias_h, bias), (key, key_v), (value, value_v), (taps_h, taps),
        (head_in4_h, head_in4), (turn4_h, turn4), (tail_in_h, tail_in),
        (block_in_h, block_in), (shift_h, shift), (block_out_h, block_out),
        (tail_out_h, tail_out), (turn2_h, turn2), (head_in2_h, head_in2), (head_out2_h, head_out2), (head_out4_h, head_out4),
    ]
    loads = [pltpu.make_async_copy(a, b, load_sem.at[i]) for i, (a, b) in enumerate(loads)]
    for load in loads:
        load.start()
    drains = []
    pend = {}
    (l_filt, l_bias, l_key, l_value, l_taps, l_hi, l_turn, l_ti, l_bi, l_sh, l_bo, l_to, l_t2, l_hi2, l_ho2, l_ho4) = loads

    l_filt.wait()
    l_bias.wait()
    for c in range(4):
        rows_f[c] = filt_v[pl.ds(c, 64, stride=4), :]
    first = jnp.where((lax.broadcasted_iota(jnp.int32, (1, 128), 1) == 0) & (seq == 0), 1.0, 0.0)
    for c in range(4):
        rows_f[c, 0:1, :] = rows_f[c, 0:1, :] + first * bias[c]

    l_key.wait()
    l_value.wait()
    l_taps.wait()
    for i, source in enumerate((key_v, value_v)):
        for c in range(4):
            ends_s[c, i : i + 1, :] = source[252 + c : 253 + c, :]
            ends_s[c, 2 + i : 3 + i, :] = source[c : c + 1, :]
    row = lax.broadcasted_iota(jnp.int32, (8, 128), 0) % 4
    lanes = lax.broadcasted_iota(jnp.int32, (256, 128), 1)

    def tap_rows(j, i):
        t = [taps[j, i, c] for c in range(4)]
        return jnp.where(row < 2, jnp.where(row == 0, t[0], t[1]), jnp.where(row == 2, t[2], t[3]))

    def short(source, i):
        x = source[...]
        result = None
        for j in range(3):
            t = tap_rows(j, i)
            moved = x
            if j > 0:
                near = pltpu.roll(x, j, 1)
                moved = jnp.where(lanes < j, pltpu.roll(near, 4, 0), near)
            term = t[None] * moved.reshape(32, 8, 128)
            result = term if result is None else result + term
        return result

    gate[...] = (short(key_v, 0) * short(value_v, 1)).reshape(256, 128)
    for c in range(4):
        rows_s[c] = gate[pl.ds(c, 64, stride=4), :]

    pl.semaphore_wait(barrier, 16)

    for i in (2, 3, 1):
        to = (zh + i) % 4
        pltpu.make_async_remote_copy(
            src_ref=ends_s.at[to],
            dst_ref=ends_z.at[zh],
            send_sem=ends_send.at[0],
            recv_sem=ends_recv.at[0],
            device_id=z_device(to * 2 + ch),
            device_id_type=MESH,
        ).start()
    drains.append(total(ends_s.at[0:3], ends_send.at[0]).wait)

    def z_exchange(f):
        for i in (2, 3, 1):
            to = (zh + i) % 4
            pltpu.make_async_remote_copy(
                src_ref=rows[f].at[to],
                dst_ref=zbuf[f].at[4 - i],
                send_sem=z_send.at[f],
                recv_sem=z_recv.at[f, 4 - i],
                device_id=z_device(to * 2 + ch),
                device_id_type=MESH,
            ).start()
            pend['z',f,4-i] = total(zbuf[f].at[4 - i], z_recv.at[f, 4 - i])
        drains.append(lambda: total(rows[f].at[0:3], z_send.at[f]).wait())

    z_exchange(0)
    z_exchange(1)
    for k in range(3):
        for _, peer in plane_peers(NEAR):
            pl.semaphore_signal(widen.at[k], inc=1, device_id=peer, device_id_type=MESH)
        pl.semaphore_wait(widen.at[k], 9)
    ends_z[zh] = ends_s[zh]
    total(ends_z.at[0:3], ends_recv.at[0]).wait()

    @pl.loop(0, 4)
    def _(block):
        after = (y * 32 + block * 8 + s + 1) % 128
        pltpu.make_async_remote_copy(
            src_ref=ends_z.at[block],
            dst_ref=ends_r.at[(after // 8) % 4],
            send_sem=ends_send.at[1],
            recv_sem=ends_recv.at[1],
            device_id={"seq": (after // 32) * 32 + zh * 8 + after % 8, "ch": ch},
            device_id_type=MESH,
        ).start()

    pend['e'] = total(ends_r, ends_recv.at[1])
    drains.append(total(ends_z, ends_send.at[1]).wait)

    def first_rows():
        pend.pop('e').wait()
        lane = lax.broadcasted_iota(jnp.int32, (4, 128), 1)
        origin = lax.broadcasted_iota(jnp.int32, (4, 128), 0) + me == 0

        def whole(i):
            x = jnp.concatenate([ends_z[b, 2 + i : 3 + i, :] for b in range(4)], axis=0)
            before = jnp.concatenate([ends_r[b, i : i + 1, :] for b in range(4)], axis=0)
            before = jnp.where(origin, 0.0, before)
            result = taps[0, i, zh] * x
            for j in (1, 2):
                moved = jnp.where(lane < j, pltpu.roll(before, j, 1), pltpu.roll(x, j, 1))
                result = result + taps[j, i, zh] * moved
            return result

        fixed = whole(0) * whole(1)
        for b in range(4):
            starts[b, 0:1, :] = fixed[b : b + 1, :]

    for f in range(2):
        zbuf[f][0] = rows[f][zh]

    def forward(f, p):
        which = FORWARD[f][p]
        count = len(which)
        head_in, turn = (head_in2, turn2) if count == 2 else (head_in4, turn4)
        for d, half in which:
            if ('z', f, d) in pend:
                pend.pop(('z',f,d)).wait()
            if f == 1 and half == 0:
                if 'e' in pend:
                    first_rows()
                zbuf_s[d, 0:1, :] = starts[(zh + d) % 4, 0:1, :]
        blocks = [zbuf[f][d, 32 * half : 32 * half + 32, :] for d, half in which]
        right = right_a.at[0 : 96 * count]
        put_split(right, jnp.concatenate(blocks, axis=0), 0)
        if f == 0 and p == 1:
            l_hi.wait()
            l_turn.wait()
        both = mm(head_in[...], right[...])
        real, imag = both[0 : 32 * count], both[32 * count : 64 * count]
        if f == 0 and p == 0:
            l_ti.wait()
        c, sn = turn[:, 0:128], turn[:, 128:256]
        turned = jnp.concatenate([real * c + imag * sn, imag * c - real * sn], axis=1)
        left = left_b.at[0 : 32 * count]
        put_split(left, turned, 1)
        spread = mm(left[...], tail_in[...])
        for b in range(count):
            for i in range(2):
                sbuf[f][p][:, 2 * b + i, :] = spread[32 * b : 32 * b + 32, 128 * i : 128 * i + 128]
        for d, peer in plane_peers():
            pltpu.make_async_remote_copy(
                src_ref=sbuf[f][p].at[d],
                dst_ref=rbuf[f][p].at[me],
                send_sem=xy_send.at[f, p],
                recv_sem=xy_recv.at[f, p],
                device_id=peer,
                device_id_type=MESH,
            ).start()
        rbuf[f][p][me] = sbuf[f][p][me]
        pend['x',f,p] = total(rbuf[f][p].at[0:31], xy_recv.at[f, p])
        drains.append(lambda: total(sbuf[f][p].at[0:31], xy_send.at[f, p]).wait())

    top_row = lax.broadcasted_iota(jnp.int32, (128, 128), 0) == 0
    sign = jnp.where(me % 2 == 0, 1.0, -1.0)

    def times(a, b):
        return a[0] * b[0] - a[1] * b[1], a[0] * b[1] + a[1] * b[0]

    def across(f):
        for p in range(len(FORWARD[f])):
            pend.pop(('x',f,p)).wait()
            for n, (d, half) in enumerate(FORWARD[f][p]):
                pair = [rbuf[f][p][:, 2 * n + i, :] for i in range(2)]
                pair = jnp.concatenate(pair, axis=1)
                high = pair.astype(BF16)
                low = (pair - high.astype(F32)).astype(BF16)
                base = (zh + d) % 4 * 64 + half * 32
                for k, part in enumerate((high, low, high)):
                    right_q[pl.ds(pl.multiple_of(base + 256 * k, 32), 32), :] = part
        if f == 0:
            l_bi.wait()
            l_sh.wait()
        for m in range(0, 256, 128):
            part = slice(m, m + 128)
            cosines = mm(block_in[part, :], right_q[...])
            sines = mm(block_in[256 + m : 384 + m, :], right_q[...])
            cre, cim, sre, sim = cosines[:, 0:128], cosines[:, 128:256], sines[:, 0:128], sines[:, 128:256]

            def alone(first, other):
                return jnp.where(top_row, first, other) if m == 0 else other

            up = alone(cre, cre + sim), alone(cim, cim - sre)
            down = alone(sre, cre - sim), alone(sim, cim + sre)
            if f == 0:
                tilt = sign * shift[part, 0:128]
                up = times(up, (1.0 + tilt, sign * shift[part, 128:256]))
                down = times(down, (1.0 - tilt, sign * shift[part, 256:384]))
                for k, x in enumerate(up + down):
                    spec[part, 128 * k : 128 * k + 128] = x
            else:
                up = times(up, (spec[part, 0:128], spec[part, 128:256]))
                down = times(down, (spec[part, 256:384], spec[part, 384:512]))
                even = [alone(up[k], up[k] + down[k]) for k in range(2)]
                odd = [alone(down[0], down[1] - up[1]), alone(down[1], up[0] - down[0])]
                for at, pair in ((m, even), (256 + m, odd)):
                    pair = jnp.concatenate(pair, axis=1)
                    high = pair.astype(BF16)
                    low = (pair - high.astype(F32)).astype(BF16)
                    for k, x in enumerate((high, low, high)):
                        right_i[512 * k + at : 512 * k + at + 128, :] = x

    l_t2.wait()
    l_hi2.wait()
    for f in range(2):
        for p in range(len(FORWARD[f])):
            forward(f, p)
    for load in (l_bo, l_to, l_ho2, l_ho4):
        load.wait()
    across(0)
    across(1)

    def send_back(p):
        low, count = 32 * BACK_START[p], len(BACK[p])
        both = mm(block_out[low : low + 32 * count, :], right_i[...])
        for n in range(count):
            for i in range(2):
                back_s[p][:, 2 * n + i, :] = both[32 * n : 32 * n + 32, 128 * i : 128 * i + 128]
        for d, peer in plane_peers():
            pltpu.make_async_remote_copy(
                src_ref=back_s[p].at[d],
                dst_ref=back_r[p].at[me],
                send_sem=back_send.at[p],
                recv_sem=back_recv.at[p],
                device_id=peer,
                device_id_type=MESH,
            ).start()
        back_r[p][me] = back_s[p][me]
        pend['b',p] = total(back_r[p].at[0:31], back_recv.at[p])
        drains.append(lambda: total(back_s[p].at[0:31], back_send.at[p]).wait())

    for p in range(len(BACK)):
        send_back(p)
    channel = ch * 4 + zh

    def finish_blocks(p):
        count = len(BACK[p])
        turn, head_out = (turn2, head_out2) if count == 2 else (turn4, head_out4)
        pend.pop(('b',p)).wait()
        high_low = []
        for i in range(2):
            for n in range(count):
                part = back_r[p][:, 2 * n + i, :]
                high = part.astype(BF16)
                low = (part - high.astype(F32)).astype(BF16)
                for k, piece in enumerate((high, low, high)):
                    left_o[32 * n : 32 * n + 32, 256 * k + 128 * i : 256 * k + 128 * i + 128] = piece
        mixed = mm(left_o[0 : 32 * count, :], tail_out[...])
        c, sn = turn[:, 0:128], turn[:, 128:256]
        real, imag = mixed[:, 0:128], mixed[:, 128:256]
        right = right_o.at[0 : 192 * count]
        put_split(right, jnp.concatenate([real * c - imag * sn, real * sn + imag * c], axis=0), 0)
        low = 32 * BACK_START[p]
        done_s[low : low + 32 * count, :] = mm(head_out[...], right[...])
        for n, to in enumerate(BACK[p]):
            block = done_s.at[low + 32 * n : low + 32 * n + 32]

            @pl.when(to == z)
            def _():
                pltpu.make_async_copy(block, out.at[tile(channel, 32)], done_recv).start()

            @pl.when(to != z)
            def _():
                pltpu.make_async_remote_copy(
                    src_ref=block,
                    dst_ref=out.at[tile(channel, 32)],
                    send_sem=done_send,
                    recv_sem=done_recv,
                    device_id=z_device(to),
                    device_id_type=MESH,
                ).start()

    for p in range(len(BACK)):
        finish_blocks(p)
    for drain in drains:
        drain()
    total(done_s.at[0:224], done_send).wait()
    total(out, done_recv).wait()


def mix(conv, query, out, conv_v, query_v, out_v, sem):
    loads, stores = [], []
    for k in range(4):
        lanes = pl.ds(1024 * k, 1024)
        loads.append((
            pltpu.make_async_copy(conv.at[:, 8 * k : 8 * k + 8], conv_v.at[k], sem.at[0, k]),
            pltpu.make_async_copy(query.at[:, lanes], query_v.at[:, lanes], sem.at[1, k]),
        ))
        stores.append(pltpu.make_async_copy(out_v.at[:, lanes], out.at[:, lanes], sem.at[2, k]))
        for load in loads[k]:
            load.start()
    for k in range(4):
        for load in loads[k]:
            load.wait()
        for j in range(8):
            lanes = slice(1024 * k + 128 * j, 1024 * k + 128 * j + 128)
            out_v[:, lanes] = conv_v[k, :, j, :] * query_v[:, lanes]
        stores[k].start()
    for store in stores:
        store.wait()


def by_time(x):
    return x.reshape(4, 64, 128).transpose(1, 0, 2).reshape(256, 128)


def local(query, key, value, filters, short_taps, bias):
    tables = make_tables()
    vm = pltpu.VMEM
    dma = pltpu.SemaphoreType.DMA
    table_scratch = [vm(t.shape, t.dtype) for t in tables]
    conv = pl.pallas_call(
        kernel,
        out_shape=jax.ShapeDtypeStruct((256, 128), F32),
        in_specs=[pl.BlockSpec(memory_space=pl.ANY)] * 16,
        out_specs=pl.BlockSpec(memory_space=pl.ANY),
        scratch_shapes=[vm((256, 128), F32)] * 3
        + [pltpu.SMEM((3, 2, 4), F32), pltpu.SMEM((4,), F32)]
        + table_scratch
        + [
            vm((256, 128), F32),
            vm((4, 8, 128), F32),
            vm((4, 8, 128), F32),
            vm((4, 8, 128), F32),
            vm((4, 8, 128), F32),
            vm((4, 64, 128), F32),
            vm((4, 64, 128), F32),
            vm((4, 64, 128), F32),
            vm((4, 64, 128), F32),
            [[vm((32, 2 * len(p), 128), F32) for p in pieces] for pieces in FORWARD],
            [[vm((32, 2 * len(p), 128), F32) for p in pieces] for pieces in FORWARD],
            vm((256, 512), F32),
            [vm((32, 2 * len(p), 128), F32) for p in BACK],
            [vm((32, 2 * len(p), 128), F32) for p in BACK],
            vm((256, 128), F32),
            vm((384, 128), BF16),
            vm((128, 768), BF16),
            vm((768, 256), BF16),
            vm((1536, 256), BF16),
            vm((128, 768), BF16),
            vm((768, 128), BF16),
            dma((16,)),
            dma((2,)), dma((2,)),
            dma((2,)), dma((2, 4)),
            dma((2, 3)), dma((2, 3)),
            dma((len(BACK),)), dma((len(BACK),)),
            dma(()), dma(()),
            pltpu.SemaphoreType.REGULAR((3,)),
        ],
        compiler_params=pltpu.CompilerParams(
            collective_id=0, has_side_effects=True, vmem_limit_bytes=56 * 1024 * 1024
        ),
        name="long_convolution",
    )(
        by_time(key), by_time(value), by_time(filters), short_taps.transpose(2, 0, 1), bias,
        *[jnp.asarray(t) for t in tables],
    )
    return pl.pallas_call(
        mix,
        out_shape=jax.ShapeDtypeStruct((8, 4096), F32),
        in_specs=[pl.BlockSpec(memory_space=pl.ANY)] * 2,
        out_specs=pl.BlockSpec(memory_space=pl.ANY),
        scratch_shapes=[vm((4, 8, 8, 128), F32), vm((8, 4096), F32), vm((8, 4096), F32), dma((3, 4))],
        compiler_params=pltpu.CompilerParams(vmem_limit_bytes=56 * 1024 * 1024),
        name="mix",
    )(conv.reshape(8, 32, 128), query)


def solution(mesh):
    return jax.shard_map(
        local,
        mesh=mesh,
        in_specs=(
            P(None, ("seq", "ch")),
            P("ch", "seq"),
            P("ch", "seq"),
            P("ch", "seq"),
            P(None, "ch", None),
            P("ch"),
        ),
        out_specs=P(None, ("seq", "ch")),
        check_vma=False,
    )
```
